32 devices in a mesh: rows: 4 (over z), feat: 8 (over y, x, core).
Axes of the slice: x: 2, y: 2, z: 4, core: 2. Of those that a mesh axis runs over, the one named last changes fastest.
Arguments:
- bins: int32 [65536, 256], P(('rows', 'feat')), may hold values from 0 to 15
- node_of: int32 [65536], P(('rows', 'feat')), may hold values from 0 to 64
- weight: float32 [65536], P(('rows', 'feat')), may hold values from 0.25 to 4
- label: float32 [65536], P(('rows', 'feat')), may hold values from -6 to 6
- split_bins: int32 [64, 256], P('rows', 'feat'), may hold values from 0 to 14
Outputs:
- gain: float32 [64, 256], P('rows', 'feat')
- node_best: float32 [64], P('rows')
The draws below stay inside these ranges and needn't reach their ends.
All inputs are finite; a program needn't handle non-finite values.
Results may differ from the reference program's by a relative error of at most 0.0035.
Values sent between devices are 32-bit elements; how exact they have to be, the bound alone decides.
No kernel may reach another device: no remote copies, remote signals or barrier semaphores. Data moves between devices by JAX's collectives and lax.ppermute only.
A program may use at most 64 MiB of HBM per device.

```python
import math
import jax
import jax.numpy as jnp
import numpy as np
from jax import lax

F = 256
B = 16
NODES = 64
ROWS = 65536


def touch_ends(result, stream_key, smallest, largest):
    shape = result.shape
    spot = [jax.random.randint(jax.random.fold_in(stream_key, axis), (), 0, shape[axis]) for axis in range(len(shape))]
    result = result.at[tuple(spot)].set(smallest)
    longest = shape.index(max(shape))
    spot[longest] = (spot[longest] + 1) % shape[longest]
    return result.at[tuple(spot)].set(largest)


def block_levels(key, extent, cuts, least, top_value):
    factor_of, own = 1.0, jax.random.fold_in(key, 6)
    for axis_at, shards_of in cuts:
        heights = jnp.exp(jax.random.uniform(jax.random.fold_in(own, axis_at), (shards_of,), jnp.float32, least / len(cuts), top_value / len(cuts)))
        factor_of = factor_of * jnp.repeat(heights, extent[axis_at] // shards_of).reshape([-1 if axis == axis_at else 1 for axis in range(len(extent))])
    return factor_of


def cumulative_ranks(count, slope):
    loads = [(1 << 20) // math.isqrt(rank ** slope) + 1 for rank in range(1, count + 1)]
    width = 1 + sum(loads) // (1 << 30)
    return np.cumsum(np.array([max(1, weight // width) for weight in loads]))


def skewed_ids(key, extent, amount, skew):
    listing = cumulative_ranks(amount, skew)
    lot = jax.random.randint(jax.random.fold_in(key, 1), extent, 0, int(listing[amount - 1]))
    standing = jnp.searchsorted(jnp.asarray(listing, jnp.int32), lot, side="right")
    return jax.random.permutation(jax.random.fold_in(key, 2), amount)[standing].astype(jnp.int32)


def noise(key, dims, spread, bound, cuts=(), kind=jnp.bfloat16):
    values = spread * jax.random.normal(key, dims, jnp.float32)
    if cuts:
        values = values * block_levels(key, dims, cuts, -0.22, 0.18)
    return jnp.clip(values, -bound, bound).astype(kind)


def setup_inputs(seed: int = 0) -> dict:
    splits = jax.random.split(jax.random.key(seed), 6)
    return {
        "bins": touch_ends(jax.random.randint(splits[0], (ROWS, F), 0, B), jax.random.fold_in(splits[0], 1), 0, B - 1).astype(jnp.int32),
        "node_of": touch_ends(skewed_ids(splits[1], (ROWS,), NODES + 1, 2), jax.random.fold_in(splits[1], 3), 0, NODES).astype(jnp.int32),
        "weight": jnp.clip(jnp.exp(math.log(4.0) - 2.7725887 * jax.random.uniform(splits[2], (ROWS,), jnp.float32) ** block_levels(splits[2], (ROWS,), ((0, 32),), -0.2, 0.2)), 0.25, 4.0),
        "label": noise(splits[3], (ROWS,), 1.0, 6.0, ((0, 32),), jnp.float32),
        "split_bins": touch_ends(jax.random.randint(splits[4], (NODES, F), 0, B - 1), jax.random.fold_in(splits[4], 1), 0, (B - 1) - 1).astype(jnp.int32),
    }


def reference(bins, node_of, weight, label, split_bins):
    w16 = weight.astype(jnp.bfloat16).astype(jnp.float32)
    wy16 = (weight * label).astype(jnp.bfloat16).astype(jnp.float32)
    vals = jnp.stack([w16, wy16], axis=1)

    def one_feature(column):
        index = node_of * B + column
        return jax.ops.segment_sum(vals, index, num_segments=(NODES + 1) * B)[: NODES * B]

    per_feature = lax.map(one_feature, bins.T)
    hist = per_feature.reshape(F, NODES, B, 2).transpose(3, 1, 0, 2)
    total = jnp.sum(hist, axis=-1)
    mask = (jnp.arange(B, dtype=jnp.int32)[None, None, :] <= split_bins[:, :, None]).astype(jnp.float32)
    left = jnp.sum(hist * mask[None], axis=-1)
    right = total - left
    gain = (left[1] ** 2 / (left[0] + 1.0) + right[1] ** 2 / (right[0] + 1.0) - total[1] ** 2 / (total[0] + 1.0)) / (total[0] + 1.0)
    return gain, jnp.max(gain, axis=1)
```

```python
import jax
import jax.numpy as jnp
from jax import lax
from jax.sharding import Mesh, PartitionSpec as P

ALL = ("rows", "chip", "core")


def shards(bins, node_of, weight, label, split_bins):
    n_rows = lax.axis_size("rows")
    n_chip = lax.axis_size("chip")
    n_all = n_rows * n_chip * 2
    core = lax.axis_index("core")
    rows_here, feats = bins.shape
    node_part, feat_part = split_bins.shape
    nodes = node_part * n_rows
    half_f = feats // 2
    half_n = node_part // 2
    w16 = weight.astype(jnp.bfloat16)
    wy16 = (weight * label).astype(jnp.bfloat16)
    node_hot = jnp.arange(nodes, dtype=jnp.int32)[:, None] == node_of[None, :]
    zero = jnp.bfloat16(0)
    sides = jnp.concatenate(
        [jnp.where(node_hot, w16[None], zero), jnp.where(node_hot, wy16[None], zero)], axis=0
    )
    total_here = jnp.sum(sides.astype(jnp.float32), axis=1)

    block = jnp.concatenate([split_bins.reshape(-1).astype(jnp.float32), total_here])
    got = lax.all_to_all(
        jnp.broadcast_to(block[None], (n_all, block.shape[0])), ALL, 0, 0, tiled=True
    )
    total = jnp.sum(got[:, node_part * feat_part :], axis=0).reshape(2, nodes)
    splits = (
        got[:, : node_part * feat_part]
        .reshape(n_rows, n_chip * 2, node_part, feat_part)
        .transpose(0, 2, 1, 3)
        .reshape(nodes, feats)
        .astype(jnp.bfloat16)
    )

    row_split = lax.dot_general(
        node_hot.astype(jnp.bfloat16), splits, (((0,), (0,)), ((), ())),
        preferred_element_type=jnp.float32,
    )
    mask = (bins.astype(jnp.float32) <= row_split).astype(jnp.bfloat16)
    left = jnp.dot(sides, mask, preferred_element_type=jnp.float32)

    pair = [(0, 1), (1, 0)]
    mine = lax.dynamic_slice_in_dim(left, core * half_f, half_f, 1)
    other = lax.dynamic_slice_in_dim(left, (1 - core) * half_f, half_f, 1)
    mine = mine + lax.ppermute(other, "core", pair)

    parts = mine.reshape(2, n_rows, 2, half_n, half_f).transpose(1, 2, 0, 3, 4)
    parts = jnp.broadcast_to(
        parts[:, None], (n_rows, n_chip, 2, 2, half_n, half_f)
    ).reshape(n_all, 2, half_n, half_f)
    parts = lax.all_to_all(parts, ALL, 0, 0, tiled=True)
    left = jnp.sum(parts.reshape(n_rows * n_chip, 2, 2, half_n, half_f), axis=0)
    left = left.transpose(1, 2, 0, 3).reshape(2, half_n, feats)

    first = lax.axis_index("rows") * node_part + core * half_n
    total = lax.dynamic_slice_in_dim(total, first, half_n, 1)[:, :, None]
    right = total - left
    gain = (
        left[1] ** 2 / (left[0] + 1.0)
        + right[1] ** 2 / (right[0] + 1.0)
        - total[1] ** 2 / (total[0] + 1.0)
    ) / (total[0] + 1.0)
    theirs = lax.ppermute(gain, "core", pair)
    gain = jnp.where(
        core == 0, jnp.concatenate([gain, theirs]), jnp.concatenate([theirs, gain])
    )
    own = (lax.axis_index("chip") * 2 + core) * feat_part
    return lax.dynamic_slice_in_dim(gain, own, feat_part, 1), jnp.max(gain, axis=1)


def solution(mesh):
    n_rows, n_feat = mesh.devices.shape
    cores = Mesh(mesh.devices.reshape(n_rows, n_feat // 2, 2), ALL)
    placed = (P(ALL, None), P(ALL), P(ALL), P(ALL), P("rows", ("chip", "core")))
    return jax.shard_map(
        shards,
        mesh=cores,
        in_specs=placed,
        out_specs=(P("rows", ("chip", "core")), P("rows")),
        check_vma=False,
    )
```

```python
import jax
import jax.numpy as jnp
from jax import lax
from jax.experimental import pallas as pl
from jax.experimental.pallas import tpu as pltpu
from jax.sharding import Mesh, PartitionSpec as P

ALL = ("rows", "chip", "core")
LANES = 128
TILE = 8
PARTS = 4
VMEM = pl.BlockSpec(memory_space=pltpu.VMEM)
HBM = pl.BlockSpec(memory_space=pltpu.HBM)


def call(kernel, outs, *args, place=VMEM, scratch=()):
    if place is HBM:
        args = [pltpu.with_memory_space_constraint(x, pltpu.HBM) for x in args]
    size = sum(x.size * x.dtype.itemsize for x in (*args, *outs))
    return pl.pallas_call(
        kernel,
        out_shape=outs,
        in_specs=[place] * len(args),
        out_specs=tuple([VMEM] * len(outs)),
        scratch_shapes=list(scratch),
        compiler_params=pltpu.CompilerParams(vmem_limit_bytes=16 << 20),
        cost_estimate=pl.CostEstimate(flops=0, bytes_accessed=size, transcendentals=0),
    )(*args)


def f32(*shape):
    return jax.ShapeDtypeStruct(shape, jnp.float32)


def bf16(*shape):
    return jax.ShapeDtypeStruct(shape, jnp.bfloat16)


def announce(nodes, groups, lines, bins_hbm, node_hbm, weight_hbm, label_hbm, split_hbm,
             out_ref, sides_ref, hot_ref, bins_ref, node_ref, weight_ref, label_ref, split_ref, sems):
    copies = [
        pltpu.make_async_copy(src, dst, sems.at[k])
        for k, (src, dst) in enumerate(
            ((node_hbm, node_ref), (weight_hbm, weight_ref), (label_hbm, label_ref),
             (split_hbm, split_ref))
        )
    ]
    for c in copies:
        c.start()
    part = bins_ref.shape[0] // PARTS
    slabs = [
        pltpu.make_async_copy(
            bins_hbm.at[pl.ds(k * part, part)], bins_ref.at[pl.ds(k * part, part)],
            sems.at[4 + k],
        )
        for k in range(PARTS)
    ]
    for c in slabs:
        c.start()
    for c in copies:
        c.wait()
    node = node_ref[...]
    weight = weight_ref[...]
    w16 = weight.astype(jnp.bfloat16).astype(jnp.float32)
    wy16 = (weight * label_ref[...]).astype(jnp.bfloat16).astype(jnp.float32)
    hot = lax.broadcasted_iota(jnp.int32, (nodes, node.shape[1]), 0) == node
    hot_ref[...] = jnp.where(hot, 1.0, 0.0).astype(jnp.bfloat16)
    sides = jnp.concatenate(
        [jnp.where(hot, w16, 0.0), jnp.where(hot, wy16, 0.0)], axis=0
    ).astype(jnp.bfloat16)
    sides_ref[...] = sides
    ones = jnp.ones((TILE, sides.shape[1]), jnp.bfloat16)
    total = lax.dot_general(
        ones, sides, (((1,), (1,)), ((), ())), preferred_element_type=jnp.float32
    )
    split = split_ref[...].astype(jnp.float32)
    held = split.shape[0] // groups
    packed = jnp.concatenate(
        [split[g * held : (g + 1) * held] for g in range(groups)], axis=1
    )
    if packed.shape[1] < LANES:
        packed = jnp.concatenate(
            [packed, jnp.zeros((held, LANES - packed.shape[1]), jnp.float32)], axis=1
        )
    block = jnp.concatenate([packed, total[:1]], axis=0)
    some = jnp.concatenate([block] * TILE, axis=0)
    for k in range(out_ref.shape[0] // some.shape[0]):
        out_ref[k * some.shape[0] : (k + 1) * some.shape[0]] = some
    for c in slabs:
        c.wait()


def partial_left(n_rows, n_feat, groups, held, feat_part, got_ref, bins_ref,
                 sides_ref, hot_ref, keep_ref, send_ref, total_ref):
    lines = held + 1
    layers = []
    for z in range(n_rows):
        cols = [
            got_ref[(z * n_feat + i) * lines : (z * n_feat + i) * lines + held]
            for i in range(n_feat)
        ]
        layers += [
            jnp.concatenate([c[:, g * feat_part : (g + 1) * feat_part] for c in cols], axis=1)
            for g in range(groups)
        ]
    splits = jnp.concatenate(layers, axis=0).astype(jnp.bfloat16)
    total_ref[...] = jnp.sum(
        got_ref[pl.ds(held, n_rows * n_feat, lines)], axis=0, keepdims=True
    )
    one, zero = jnp.bfloat16(1), jnp.bfloat16(0)
    rows, step = bins_ref.shape[0], 256
    left = jnp.zeros((sides_ref.shape[0], bins_ref.shape[1]), jnp.float32)
    for r in range(0, rows, step):
        row_split = lax.dot_general(
            hot_ref[:, r : r + step], splits, (((0,), (0,)), ((), ())),
            preferred_element_type=jnp.float32,
        )
        mask = jnp.where(
            bins_ref[r : r + step].astype(jnp.float32) <= row_split, 1.0, 0.0
        ).astype(jnp.bfloat16)
        left += jnp.dot(sides_ref[:, r : r + step], mask, preferred_element_type=jnp.float32)
    half = left.shape[1] // 2
    low, high = left[:, :half], left[:, half:]
    first = lax.axis_index("core") == 0
    keep_ref[...] = jnp.where(first, low, high)
    send_ref[...] = jnp.where(first, high, low)


def spread(n_rows, n_chip, half_n, keep_ref, recv_ref, out_ref):
    both = keep_ref[...] + recv_ref[...]
    nodes = both.shape[0] // 2
    for z in range(n_rows):
        for c in range(2):
            at = (z * 2 + c) * half_n
            tile = jnp.concatenate(
                [both[at : at + half_n], both[nodes + at : nodes + at + half_n]], axis=0
            )
            for chip in range(n_chip):
                out_ref[(z * n_chip + chip) * 2 + c] = tile


def split_gain(half_n, node_part, part_ref, total_ref, gain_ref):
    left = jnp.sum(part_ref[...], axis=0)
    left0 = jnp.concatenate([left[0, :half_n], left[1, :half_n]], axis=1)
    left1 = jnp.concatenate([left[0, half_n:], left[1, half_n:]], axis=1)
    row = total_ref[...]
    where = lax.axis_index("rows") * node_part + lax.axis_index("core") * half_n
    lane = lax.broadcasted_iota(jnp.int32, (half_n, LANES), 1)
    at = lax.broadcasted_iota(jnp.int32, (half_n, LANES), 0) + where
    total0 = jnp.sum(jnp.where(lane == at, row, 0.0), axis=1, keepdims=True)
    total1 = jnp.sum(jnp.where(lane == at + LANES // 2, row, 0.0), axis=1, keepdims=True)
    right0 = total0 - left0
    right1 = total1 - left1
    gain_ref[...] = (
        left1 * left1 / (left0 + 1.0)
        + right1 * right1 / (right0 + 1.0)
        - total1 * total1 / (total0 + 1.0)
    ) / (total0 + 1.0)


def finish(gain_ref, theirs_ref, out_ref, best_ref):
    mine, theirs = gain_ref[...], theirs_ref[...]
    first = lax.axis_index("core") == 0
    gain = jnp.concatenate(
        [jnp.where(first, mine, theirs), jnp.where(first, theirs, mine)], axis=0
    )
    n = gain.shape[0]
    best = jnp.max(gain, axis=1, keepdims=True)
    eye = lax.broadcasted_iota(jnp.int32, (n, n), 0) == lax.broadcasted_iota(jnp.int32, (n, n), 1)
    best_ref[...] = jnp.sum(jnp.where(eye, best, 0.0), axis=0, keepdims=True)
    feats, width = gain.shape[1], out_ref.shape[1]
    own = (lax.axis_index("chip") * 2 + lax.axis_index("core")) * width
    turned = pltpu.roll(gain, lax.rem(feats - own, feats), 1)
    out_ref[...] = turned[:, : out_ref.shape[1]]


def shards(bins, node_of, weight, label, split_bins):
    n_rows = lax.axis_size("rows")
    n_chip = lax.axis_size("chip")
    n_all = n_rows * n_chip * 2
    rows_here, feats = bins.shape
    node_part, feat_part = split_bins.shape
    nodes = node_part * n_rows
    half_f = feats // 2
    half_n = node_part // 2
    groups = min(LANES // feat_part, node_part)
    held = node_part // groups
    lines = held + 1

    per_row = [x.reshape(1, rows_here) for x in (node_of, weight, label)]
    def k_announce(*refs):
        announce(nodes, groups, lines, *refs)
    block, sides, hot, bins = call(
        k_announce,
        [f32(n_all * lines, LANES), bf16(2 * nodes, rows_here), bf16(nodes, rows_here),
         jax.ShapeDtypeStruct(bins.shape, jnp.int32)],
        bins, *per_row, split_bins, place=HBM,
        scratch=[
            pltpu.VMEM((1, rows_here), jnp.int32),
            pltpu.VMEM((1, rows_here), jnp.float32),
            pltpu.VMEM((1, rows_here), jnp.float32),
            pltpu.VMEM(split_bins.shape, jnp.int32),
            pltpu.SemaphoreType.DMA((4 + PARTS,)),
        ],
    )
    got = lax.all_to_all(
        block.reshape(n_all, 1, lines * LANES), ALL, 0, 0, tiled=True
    ).reshape(n_all * lines, LANES)

    def k_left(*refs):
        partial_left(n_rows, n_chip * 2, groups, held, feat_part, *refs)
    keep, send, total = call(
        k_left,
        [f32(2 * nodes, half_f), f32(2 * nodes, half_f), f32(1, LANES)],
        got, bins, sides, hot,
    )
    pair = [(0, 1), (1, 0)]
    recv = lax.ppermute(send, "core", pair)

    def k_spread(*refs):
        spread(n_rows, n_chip, half_n, *refs)
    (parts,) = call(k_spread, [f32(n_all, 2 * half_n, half_f)], keep, recv)
    parts = lax.all_to_all(parts, ALL, 0, 0, tiled=True)

    def k_gain(*refs):
        split_gain(half_n, node_part, *refs)
    (gain,) = call(
        k_gain, [f32(half_n, feats)],
        parts.reshape(n_all // 2, 2, 2 * half_n, half_f), total,
    )
    theirs = lax.ppermute(gain, "core", pair)
    out, best = call(
        finish, [f32(node_part, feat_part), f32(1, node_part)],
        gain, theirs,
    )
    return out, best.reshape(node_part)


def solution(mesh):
    n_rows, n_feat = mesh.devices.shape
    cores = Mesh(mesh.devices.reshape(n_rows, n_feat // 2, 2), ALL)
    placed = (P(ALL, None), P(ALL), P(ALL), P(ALL), P("rows", ("chip", "core")))
    return jax.shard_map(
        shards,
        mesh=cores,
        in_specs=placed,
        out_specs=(P("rows", ("chip", "core")), P("rows")),
        check_vma=False,
    )
```

```python
import math

import jax
import jax.numpy as jnp
from jax import lax
from jax.experimental import pallas as pl
from jax.experimental.pallas import tpu as pltpu
from jax.sharding import Mesh, PartitionSpec as P

ALL = ("rows", "line", "chip", "core")
FIRST = ("rows", "line", "chip", "core")
SECOND = ("line", "chip", "core", "rows")
LANES = 128
BINS = 16
PARTS = 4
STEP = 512
VMEM = pl.BlockSpec(memory_space=pltpu.VMEM)
HBM = pl.BlockSpec(memory_space=pltpu.HBM)
ANY = pl.BlockSpec(memory_space=pl.ANY)


def place_in(order, sizes, **at):
    d = 0
    for axis in order:
        d = d * sizes[axis] + at[axis]
    return d


def call(kernel, outs, *args, place=None, scratch=()):
    place = place or [VMEM] * len(args)
    args = [
        pltpu.with_memory_space_constraint(x, pltpu.HBM) if p is HBM else x
        for x, p in zip(args, place)
    ]
    size = sum(x.size * x.dtype.itemsize for x in (*args, *outs))
    return pl.pallas_call(
        kernel,
        out_shape=outs,
        in_specs=place,
        out_specs=tuple([VMEM] * len(outs)),
        scratch_shapes=list(scratch),
        compiler_params=pltpu.CompilerParams(vmem_limit_bytes=16 << 20),
        cost_estimate=pl.CostEstimate(flops=0, bytes_accessed=size, transcendentals=0),
    )(*args)


def f32(*shape):
    return jax.ShapeDtypeStruct(shape, jnp.float32)


def announce(groups, node_hbm, weight_hbm, label_hbm, split_hbm, out_ref, row_ref,
             node_ref, weight_ref, label_ref, split_ref, sems):
    copies = [
        pltpu.make_async_copy(src, dst, sems.at[k])
        for k, (src, dst) in enumerate(
            ((split_hbm, split_ref), (node_hbm, node_ref), (weight_hbm, weight_ref),
             (label_hbm, label_ref))
        )
    ]
    for c in copies:
        c.start()
    for c in copies:
        c.wait()
    split = split_ref[...].astype(jnp.float32)
    held = split.shape[0] // groups
    block = jnp.concatenate(
        [split[g * held : (g + 1) * held] for g in range(groups)], axis=1
    )
    if block.shape[1] < LANES:
        block = jnp.concatenate(
            [block, jnp.zeros((held, LANES - block.shape[1]), jnp.float32)], axis=1
        )
    many = max(1, 8 // held)
    some = jnp.concatenate([block] * many, axis=0)
    for k in range(out_ref.shape[0] // some.shape[0]):
        out_ref[k * some.shape[0] : (k + 1) * some.shape[0]] = some
    weight = weight_ref[...]
    row_ref[0:1] = node_ref[...].astype(jnp.float32)
    row_ref[1:2] = weight.astype(jnp.bfloat16).astype(jnp.float32)
    row_ref[2:3] = (weight * label_ref[...]).astype(jnp.bfloat16).astype(jnp.float32)


def histogram(nodes, bins_hbm, row_ref, far_bins, far_row, out_ref, bins_ref, sems):
    rows, half = bins_ref.shape
    part = rows // PARTS
    first = pl.multiple_of(lax.axis_index("core") * half, half)
    copies = [
        pltpu.make_async_copy(
            bins_hbm.at[pl.ds(k * part, part), pl.ds(first, half)],
            bins_ref.at[pl.ds(k * part, part)],
            sems.at[k],
        )
        for k in range(PARTS)
    ]
    for c in copies:
        c.start()

    def sides_of(ref):
        node = ref[0:1].astype(jnp.int32)
        hot = lax.broadcasted_iota(jnp.int32, (nodes, rows), 0) == node
        return jnp.concatenate(
            [jnp.where(hot, ref[1:2], 0.0), jnp.where(hot, ref[2:3], 0.0)], axis=0
        ).astype(jnp.bfloat16)

    def add(sides, bins, seed):
        one, zero = jnp.bfloat16(1), jnp.bfloat16(0)
        for b in range(0, BINS, 2):
            acc = jnp.zeros((2 * nodes, 2 * half), jnp.float32)
            for r in range(0, rows, STEP):
                chunk = bins[r : r + STEP]
                mask = jnp.concatenate(
                    [jnp.where(chunk <= jnp.bfloat16(b + k), one, zero) for k in range(2)],
                    axis=1,
                )
                acc += jnp.dot(
                    sides[:, r : r + STEP], mask, preferred_element_type=jnp.float32
                )
            for k in range(2):
                here = acc[:, k * half : (k + 1) * half]
                out_ref[b + k] = here if seed else out_ref[b + k] + here

    add(sides_of(far_row), far_bins[:, pl.ds(first, half)].astype(jnp.bfloat16), True)
    sides = sides_of(row_ref)
    for c in copies:
        c.wait()
    add(sides, bins_ref[...].astype(jnp.bfloat16), False)


def choose(sizes, groups, held, feat_part, half_n, got_ref, below_ref, out_ref):
    half = below_ref.shape[2]
    nodes = below_ref.shape[1] // 2
    mine = half // feat_part
    base = lax.axis_index("core") * mine
    n_rows, n_line, n_chip = sizes["rows"], sizes["line"], sizes["chip"]
    layers = []
    for z in range(n_rows):
        cols = []
        for i in range(mine):
            chip = (base + i) // 2
            d = place_in(
                FIRST, sizes, rows=z, line=chip // n_chip, chip=chip % n_chip, core=i % 2
            )
            cols.append(got_ref[pl.ds(d * held, held)])
        layers += [
            jnp.concatenate([c[:, g * feat_part : (g + 1) * feat_part] for c in cols], axis=1)
            for g in range(groups)
        ]
    split = jnp.concatenate(layers, axis=0)
    left0, left1 = below_ref[0, :nodes], below_ref[0, nodes:]
    for b in range(1, BINS - 1):
        further = split >= b
        left0 = jnp.where(further, below_ref[b, :nodes], left0)
        left1 = jnp.where(further, below_ref[b, nodes:], left1)
    everything = below_ref[BINS - 1]
    eye = lax.broadcasted_iota(jnp.int32, everything.shape, 0) == lax.broadcasted_iota(
        jnp.int32, everything.shape, 1
    )
    total = jnp.sum(jnp.where(eye, everything, 0.0), axis=0, keepdims=True)
    lines = 2 * half_n + 1
    for z in range(n_rows):
        for c in range(2):
            at = (z * 2 + c) * half_n
            tile = jnp.concatenate(
                [left0[at : at + half_n], left1[at : at + half_n], total], axis=0
            )
            for line in range(n_line):
                for chip in range(n_chip):
                    d = place_in(SECOND, sizes, rows=z, line=line, chip=chip, core=c)
                    out_ref[d * lines : (d + 1) * lines] = tile


def split_gain(half_n, node_part, sizes, part_ref, gain_ref):
    lines = 2 * half_n + 1
    sums = []
    for c in range(2):
        both = None
        for z in range(sizes["rows"]):
            for line in range(sizes["line"]):
                for chip in range(sizes["chip"]):
                    d = place_in(SECOND, sizes, rows=z, line=line, chip=chip, core=c)
                    one = part_ref[d * lines : (d + 1) * lines]
                    both = one if both is None else both + one
        sums.append(both)
    left0 = jnp.concatenate([s[:half_n] for s in sums], axis=1)
    left1 = jnp.concatenate([s[half_n : 2 * half_n] for s in sums], axis=1)
    row = sums[0][2 * half_n :]
    where = lax.axis_index("rows") * node_part + lax.axis_index("core") * half_n
    lane = lax.broadcasted_iota(jnp.int32, (half_n, LANES), 1)
    at = lax.broadcasted_iota(jnp.int32, (half_n, LANES), 0) + where
    total0 = jnp.sum(jnp.where(lane == at, row, 0.0), axis=1, keepdims=True)
    total1 = jnp.sum(jnp.where(lane == at + LANES // 2, row, 0.0), axis=1, keepdims=True)
    right0 = total0 - left0
    right1 = total1 - left1
    gain_ref[...] = (
        left1 * left1 / (left0 + 1.0)
        + right1 * right1 / (right0 + 1.0)
        - total1 * total1 / (total0 + 1.0)
    ) / (total0 + 1.0)


def finish(gain_ref, theirs_ref, out_ref, best_ref):
    mine, theirs = gain_ref[...], theirs_ref[...]
    first = lax.axis_index("core") == 0
    gain = jnp.concatenate(
        [jnp.where(first, mine, theirs), jnp.where(first, theirs, mine)], axis=0
    )
    n = gain.shape[0]
    best = jnp.max(gain, axis=1, keepdims=True)
    eye = lax.broadcasted_iota(jnp.int32, (n, n), 0) == lax.broadcasted_iota(jnp.int32, (n, n), 1)
    best_ref[...] = jnp.sum(jnp.where(eye, best, 0.0), axis=0, keepdims=True)
    feats, width = gain.shape[1], out_ref.shape[1]
    own = lax.axis_index(("line", "chip", "core")) * width
    turned = pltpu.roll(gain, lax.rem(feats - own, feats), 1)
    out_ref[...] = turned[:, : out_ref.shape[1]]


def shards(bins, node_of, weight, label, split_bins):
    sizes = {axis: lax.axis_size(axis) for axis in ALL}
    n_rows = sizes["rows"]
    n_all = math.prod(sizes.values())
    rows_here, feats = bins.shape
    node_part, feat_part = split_bins.shape
    nodes = node_part * n_rows
    half_f = feats // 2
    half_n = node_part // 2
    groups = min(LANES // feat_part, node_part)
    held = node_part // groups
    lines = 2 * half_n + 1
    pair = [(0, 1), (1, 0)]
    far_bins = lax.ppermute(bins, "core", pair)
    def k_announce(*refs):
        announce(groups, *refs)
    per_row = [x.reshape(1, rows_here) for x in (node_of, weight, label)]
    block, row = call(
        k_announce, [f32(n_all * held, LANES), f32(3, rows_here)], *per_row, split_bins,
        place=[HBM] * 4,
        scratch=[
            pltpu.VMEM((1, rows_here), jnp.int32),
            pltpu.VMEM((1, rows_here), jnp.float32),
            pltpu.VMEM((1, rows_here), jnp.float32),
            pltpu.VMEM(split_bins.shape, jnp.int32),
            pltpu.SemaphoreType.DMA((4,)),
        ],
    )
    got = lax.all_to_all(
        block.reshape(n_all, 1, held * LANES), FIRST, 0, 0, tiled=True
    ).reshape(n_all * held, LANES)
    far_row = lax.ppermute(row, "core", pair)

    def k_histogram(*refs):
        histogram(nodes, *refs)
    (below,) = call(
        k_histogram, [f32(BINS, 2 * nodes, half_f)], bins, row, far_bins, far_row,
        place=[HBM, VMEM, VMEM, VMEM],
        scratch=[pltpu.VMEM((rows_here, half_f), jnp.int32), pltpu.SemaphoreType.DMA((PARTS,))],
    )

    def k_choose(*refs):
        choose(sizes, groups, held, feat_part, half_n, *refs)
    (parts,) = call(k_choose, [f32(n_all * lines, half_f)], got, below)
    parts = lax.all_to_all(
        parts.reshape(n_all, 1, lines * half_f), SECOND, 0, 0, tiled=True
    ).reshape(n_all * lines, half_f)

    def k_gain(*refs):
        split_gain(half_n, node_part, sizes, *refs)
    (gain,) = call(k_gain, [f32(half_n, feats)], parts)
    other = lax.ppermute(gain, "core", pair)
    out, best = call(
        finish, [f32(node_part, feat_part), f32(1, node_part)], gain, other
    )
    return out, best.reshape(node_part)


def solution(mesh):
    n_rows, n_feat = mesh.devices.shape
    cores = Mesh(mesh.devices.reshape(n_rows, n_feat // 4, 2, 2), ALL)
    placed = (P(ALL, None), P(ALL), P(ALL), P(ALL), P("rows", ("line", "chip", "core")))
    return jax.shard_map(
        shards,
        mesh=cores,
        in_specs=placed,
        out_specs=(P("rows", ("line", "chip", "core")), P("rows")),
        check_vma=False,
    )
```

```python
import math

import jax
import jax.numpy as jnp
from jax import lax
from jax.experimental import pallas as pl
from jax.experimental.pallas import tpu as pltpu
from jax.sharding import Mesh, PartitionSpec as P

ROWS = ("far", "near")
FEAT = ("line", "chip", "core")
ALL = ROWS + FEAT
FIRST = ("far", "near", "line", "chip", "core")
SECOND = ("core", "near", "line", "chip", "far")
LANES = 128
BINS = 16
PARTS = 4
STEP = 512
VMEM = pl.BlockSpec(memory_space=pltpu.VMEM)
HBM = pl.BlockSpec(memory_space=pltpu.HBM)
ANY = pl.BlockSpec(memory_space=pl.ANY)


def place_in(order, sizes, **at):
    d = 0
    for axis in order:
        d = d * sizes[axis] + at[axis]
    return d


def call(kernel, outs, *args, place=None, where=None, scratch=()):
    place = place or [VMEM] * len(args)
    args = [
        pltpu.with_memory_space_constraint(x, pltpu.HBM) if p is HBM else x
        for x, p in zip(args, place)
    ]
    size = sum(x.size * x.dtype.itemsize for x in (*args, *outs))
    return pl.pallas_call(
        kernel,
        out_shape=outs,
        in_specs=place,
        out_specs=tuple(where or [VMEM] * len(outs)),
        scratch_shapes=list(scratch),
        compiler_params=pltpu.CompilerParams(vmem_limit_bytes=16 << 20),
        cost_estimate=pl.CostEstimate(flops=0, bytes_accessed=size, transcendentals=0),
    )(*args)


def f32(*shape):
    return jax.ShapeDtypeStruct(shape, jnp.float32)


def announce(groups, node_hbm, weight_hbm, label_hbm, split_hbm, out_ref, row_ref,
             node_ref, weight_ref, label_ref, split_ref, block_ref, sems):
    copies = [
        pltpu.make_async_copy(src, dst, sems.at[k])
        for k, (src, dst) in enumerate(
            ((split_hbm, split_ref), (node_hbm, node_ref), (weight_hbm, weight_ref),
             (label_hbm, label_ref))
        )
    ]
    for c in copies:
        c.start()
    copies[0].wait()
    split = split_ref[...].astype(jnp.float32)
    held = split.shape[0] // groups
    block = jnp.concatenate(
        [split[g * held : (g + 1) * held] for g in range(groups)], axis=1
    )
    if block.shape[1] < LANES:
        block = jnp.concatenate(
            [block, jnp.zeros((held, LANES - block.shape[1]), jnp.float32)], axis=1
        )
    many = max(1, 8 // held)
    some = jnp.concatenate([block] * many, axis=0)
    for k in range(block_ref.shape[0] // some.shape[0]):
        block_ref[k * some.shape[0] : (k + 1) * some.shape[0]] = some
    out = pltpu.make_async_copy(block_ref, out_ref, sems.at[4])
    out.start()
    for c in copies[1:]:
        c.wait()
    weight = weight_ref[...]
    row_ref[0:1] = node_ref[...].astype(jnp.float32)
    row_ref[1:2] = weight.astype(jnp.bfloat16).astype(jnp.float32)
    row_ref[2:3] = (weight * label_ref[...]).astype(jnp.bfloat16).astype(jnp.float32)
    out.wait()


def histogram(nodes, bins_hbm, row_ref, far_bins, far_row, out_ref, bins_ref, sems):
    rows, half = bins_ref.shape
    part = rows // PARTS
    first = pl.multiple_of(lax.axis_index("core") * half, half)
    copies = [
        pltpu.make_async_copy(
            bins_hbm.at[pl.ds(k * part, part), pl.ds(first, half)],
            bins_ref.at[pl.ds(k * part, part)],
            sems.at[k],
        )
        for k in range(PARTS)
    ]
    for c in copies:
        c.start()

    def sides_of(ref):
        node = ref[0:1].astype(jnp.int32)
        hot = lax.broadcasted_iota(jnp.int32, (nodes, rows), 0) == node
        return jnp.concatenate(
            [jnp.where(hot, ref[1:2], 0.0), jnp.where(hot, ref[2:3], 0.0)], axis=0
        ).astype(jnp.bfloat16)

    def add(sides, bins, seed):
        one, zero = jnp.bfloat16(1), jnp.bfloat16(0)
        for b in range(0, BINS, 2):
            acc = jnp.zeros((2 * nodes, 2 * half), jnp.float32)
            for r in range(0, rows, STEP):
                chunk = bins[r : r + STEP]
                mask = jnp.concatenate(
                    [jnp.where(chunk <= jnp.bfloat16(b + k), one, zero) for k in range(2)],
                    axis=1,
                )
                acc += jnp.dot(
                    sides[:, r : r + STEP], mask, preferred_element_type=jnp.float32
                )
            for k in range(2):
                here = acc[:, k * half : (k + 1) * half]
                out_ref[b + k] = here if seed else out_ref[b + k] + here

    add(sides_of(far_row), far_bins[:, pl.ds(first, half)].astype(jnp.bfloat16), True)
    sides = sides_of(row_ref)
    for c in copies:
        c.wait()
    add(sides, bins_ref[...].astype(jnp.bfloat16), False)


def choose(sizes, groups, held, feat_part, half_n, got_ref, below_ref, out_ref):
    half = below_ref.shape[2]
    nodes = below_ref.shape[1] // 2
    mine = half // feat_part
    base = lax.axis_index("core") * mine
    n_near, n_line, n_chip = sizes["near"], sizes["line"], sizes["chip"]
    n_rows = sizes["far"] * n_near
    layers = []
    for z in range(n_rows):
        cols = []
        for i in range(mine):
            chip = (base + i) // 2
            d = place_in(
                FIRST, sizes, far=z // n_near, near=z % n_near,
                line=chip // n_chip, chip=chip % n_chip, core=i % 2,
            )
            cols.append(got_ref[pl.ds(d * held, held)])
        layers += [
            jnp.concatenate([c[:, g * feat_part : (g + 1) * feat_part] for c in cols], axis=1)
            for g in range(groups)
        ]
    split = jnp.concatenate(layers, axis=0)
    left0, left1 = below_ref[0, :nodes], below_ref[0, nodes:]
    for b in range(1, BINS - 1):
        further = split >= b
        left0 = jnp.where(further, below_ref[b, :nodes], left0)
        left1 = jnp.where(further, below_ref[b, nodes:], left1)
    everything = below_ref[BINS - 1]
    eye = lax.broadcasted_iota(jnp.int32, everything.shape, 0) == lax.broadcasted_iota(
        jnp.int32, everything.shape, 1
    )
    total = jnp.sum(jnp.where(eye, everything, 0.0), axis=0, keepdims=True)
    lines = 2 * half_n + 1
    for z in range(n_rows):
        for c in range(2):
            at = (z * 2 + c) * half_n
            tile = jnp.concatenate(
                [left0[at : at + half_n], left1[at : at + half_n], total], axis=0
            )
            for line in range(n_line):
                for chip in range(n_chip):
                    d = place_in(
                        SECOND, sizes, far=z // n_near, near=z % n_near,
                        line=line, chip=chip, core=c,
                    )
                    out_ref[d * lines : (d + 1) * lines] = tile


def split_gain(half_n, node_part, sizes, part_ref, gain_ref):
    lines = 2 * half_n + 1
    after = math.prod(sizes[a] for a in SECOND[SECOND.index("core") + 1 :])
    sums = []
    for c in range(2):
        both = None
        for d in range(math.prod(sizes.values())):
            if (d // after) % 2 == c:
                one = part_ref[d * lines : (d + 1) * lines]
                both = one if both is None else both + one
        sums.append(both)
    left0 = jnp.concatenate([s[:half_n] for s in sums], axis=1)
    left1 = jnp.concatenate([s[half_n : 2 * half_n] for s in sums], axis=1)
    row = sums[0][2 * half_n :]
    where = lax.axis_index(ROWS) * node_part + lax.axis_index("core") * half_n
    lane = lax.broadcasted_iota(jnp.int32, (half_n, LANES), 1)
    at = lax.broadcasted_iota(jnp.int32, (half_n, LANES), 0) + where
    total0 = jnp.sum(jnp.where(lane == at, row, 0.0), axis=1, keepdims=True)
    total1 = jnp.sum(jnp.where(lane == at + LANES // 2, row, 0.0), axis=1, keepdims=True)
    right0 = total0 - left0
    right1 = total1 - left1
    gain_ref[...] = (
        left1 * left1 / (left0 + 1.0)
        + right1 * right1 / (right0 + 1.0)
        - total1 * total1 / (total0 + 1.0)
    ) / (total0 + 1.0)


def finish(gain_ref, theirs_ref, out_ref, best_ref):
    mine, theirs = gain_ref[...], theirs_ref[...]
    first = lax.axis_index("core") == 0
    gain = jnp.concatenate(
        [jnp.where(first, mine, theirs), jnp.where(first, theirs, mine)], axis=0
    )
    n = gain.shape[0]
    best = jnp.max(gain, axis=1, keepdims=True)
    eye = lax.broadcasted_iota(jnp.int32, (n, n), 0) == lax.broadcasted_iota(jnp.int32, (n, n), 1)
    best_ref[...] = jnp.sum(jnp.where(eye, best, 0.0), axis=0, keepdims=True)
    feats, width = gain.shape[1], out_ref.shape[1]
    own = lax.axis_index(FEAT) * width
    turned = pltpu.roll(gain, lax.rem(feats - own, feats), 1)
    out_ref[...] = turned[:, : out_ref.shape[1]]


def shards(bins, node_of, weight, label, split_bins):
    sizes = {axis: lax.axis_size(axis) for axis in ALL}
    n_rows = sizes["far"] * sizes["near"]
    n_all = math.prod(sizes.values())
    rows_here, feats = bins.shape
    node_part, feat_part = split_bins.shape
    nodes = node_part * n_rows
    half_f = feats // 2
    half_n = node_part // 2
    groups = min(LANES // feat_part, node_part)
    held = node_part // groups
    lines = 2 * half_n + 1
    pair = [(0, 1), (1, 0)]
    far_bins = lax.ppermute(bins, "core", pair)
    def k_announce(*refs):
        announce(groups, *refs)
    per_row = [x.reshape(1, rows_here) for x in (node_of, weight, label)]
    block, row = call(
        k_announce, [f32(n_all * held, LANES), f32(3, rows_here)], *per_row, split_bins,
        place=[HBM] * 4, where=[HBM, VMEM],
        scratch=[
            pltpu.VMEM((1, rows_here), jnp.int32),
            pltpu.VMEM((1, rows_here), jnp.float32),
            pltpu.VMEM((1, rows_here), jnp.float32),
            pltpu.VMEM(split_bins.shape, jnp.int32),
            pltpu.VMEM((n_all * held, LANES), jnp.float32),
            pltpu.SemaphoreType.DMA((5,)),
        ],
    )
    got = lax.all_to_all(
        block.reshape(n_all, 1, held * LANES), FIRST, 0, 0, tiled=True
    ).reshape(n_all * held, LANES)
    far_row = lax.ppermute(row, "core", pair)

    def k_histogram(*refs):
        histogram(nodes, *refs)
    (below,) = call(
        k_histogram, [f32(BINS, 2 * nodes, half_f)], bins, row, far_bins, far_row,
        place=[HBM, VMEM, VMEM, VMEM],
        scratch=[pltpu.VMEM((rows_here, half_f), jnp.int32), pltpu.SemaphoreType.DMA((PARTS,))],
    )

    def k_choose(*refs):
        choose(sizes, groups, held, feat_part, half_n, *refs)
    (parts,) = call(k_choose, [f32(n_all * lines, half_f)], got, below)
    parts = lax.all_to_all(
        parts.reshape(n_all, 1, lines * half_f), SECOND, 0, 0, tiled=True
    ).reshape(n_all * lines, half_f)

    def k_gain(*refs):
        split_gain(half_n, node_part, sizes, *refs)
    (gain,) = call(k_gain, [f32(half_n, feats)], parts)
    other = lax.ppermute(gain, "core", pair)
    out, best = call(
        finish, [f32(node_part, feat_part), f32(1, node_part)], gain, other
    )
    return out, best.reshape(node_part)


def solution(mesh):
    n_rows, n_feat = mesh.devices.shape
    cores = Mesh(mesh.devices.reshape(n_rows // 2, 2, n_feat // 4, 2, 2), ALL)
    placed = (P(ALL, None), P(ALL), P(ALL), P(ALL), P(ROWS, FEAT))
    return jax.shard_map(
        shards,
        mesh=cores,
        in_specs=placed,
        out_specs=(P(ROWS, FEAT), P(ROWS)),
        check_vma=False,
    )
```

```python
import math

import jax
import jax.numpy as jnp
from jax import lax
from jax.experimental import pallas as pl
from jax.experimental.pallas import tpu as pltpu
from jax.sharding import Mesh, PartitionSpec as P

ROWS = ("far", "near")
FEAT = ("line", "chip", "core")
ALL = ROWS + FEAT
FIRST = ("far", "near", "line", "chip", "core")
SECOND = ("core", "near", "line", "chip", "far")
LANES = 128
BINS = 16
PARTS = 4
STEP = 512
VMEM = pl.BlockSpec(memory_space=pltpu.VMEM)
HBM = pl.BlockSpec(memory_space=pltpu.HBM)
ANY = pl.BlockSpec(memory_space=pl.ANY)


def place_in(order, sizes, **at):
    d = 0
    for axis in order:
        d = d * sizes[axis] + at[axis]
    return d


def call(kernel, outs, *args, place=None, where=None, scratch=()):
    place = place or [VMEM] * len(args)
    args = [
        pltpu.with_memory_space_constraint(x, pltpu.HBM) if p is HBM else x
        for x, p in zip(args, place)
    ]
    size = sum(x.size * x.dtype.itemsize for x in (*args, *outs))
    return pl.pallas_call(
        kernel,
        out_shape=outs,
        in_specs=place,
        out_specs=tuple(where or [VMEM] * len(outs)),
        scratch_shapes=list(scratch),
        compiler_params=pltpu.CompilerParams(vmem_limit_bytes=16 << 20),
        cost_estimate=pl.CostEstimate(flops=0, bytes_accessed=size, transcendentals=0),
    )(*args)


def f32(*shape):
    return jax.ShapeDtypeStruct(shape, jnp.float32)


def bf16(*shape):
    return jax.ShapeDtypeStruct(shape, jnp.bfloat16)


def announce(groups, bins_hbm, node_hbm, weight_hbm, label_hbm, split_hbm, out_ref, row_ref,
             near_ref, node_ref, weight_ref, label_ref, split_ref, block_ref, sems):
    copies = [
        pltpu.make_async_copy(src, dst, sems.at[k])
        for k, (src, dst) in enumerate(
            ((split_hbm, split_ref), (node_hbm, node_ref), (weight_hbm, weight_ref),
             (label_hbm, label_ref))
        )
    ]
    rows, half = near_ref.shape
    part = rows // PARTS
    first = pl.multiple_of(lax.axis_index("core") * half, half)
    slabs = [
        pltpu.make_async_copy(
            bins_hbm.at[pl.ds(k * part, part), pl.ds(first, half)],
            near_ref.at[pl.ds(k * part, part)],
            sems.at[5 + k],
        )
        for k in range(PARTS)
    ]
    for c in copies + slabs:
        c.start()
    copies[0].wait()
    split = split_ref[...].astype(jnp.float32)
    held = split.shape[0] // groups
    block = jnp.concatenate(
        [split[g * held : (g + 1) * held] for g in range(groups)], axis=1
    )
    if block.shape[1] < LANES:
        block = jnp.concatenate(
            [block, jnp.zeros((held, LANES - block.shape[1]), jnp.float32)], axis=1
        )
    many = max(1, 8 // held)
    some = jnp.concatenate([block] * many, axis=0)
    for k in range(block_ref.shape[0] // some.shape[0]):
        block_ref[k * some.shape[0] : (k + 1) * some.shape[0]] = some
    out = pltpu.make_async_copy(block_ref, out_ref, sems.at[4])
    out.start()
    for c in copies[1:]:
        c.wait()
    weight = weight_ref[...]
    row_ref[0:1] = node_ref[...].astype(jnp.float32)
    row_ref[1:2] = weight.astype(jnp.bfloat16).astype(jnp.float32)
    row_ref[2:3] = (weight * label_ref[...]).astype(jnp.bfloat16).astype(jnp.float32)
    for c in slabs:
        c.wait()
    out.wait()


def sides_of(nodes, row_ref):
    node = row_ref[0:1].astype(jnp.int32)
    hot = lax.broadcasted_iota(jnp.int32, (nodes, node.shape[1]), 0) == node
    return jnp.concatenate(
        [jnp.where(hot, row_ref[1:2], 0.0), jnp.where(hot, row_ref[2:3], 0.0)], axis=0
    ).astype(jnp.bfloat16)


def histogram(nodes, bins_ref, row_ref, before_ref, out_ref):
    half = out_ref.shape[2]
    rows, width = bins_ref.shape
    if width == half:
        bins = bins_ref[...]
    else:
        first = pl.multiple_of(lax.axis_index("core") * half, half)
        bins = bins_ref[:, pl.ds(first, half)]
    bins = bins.astype(jnp.bfloat16)
    sides = sides_of(nodes, row_ref)
    one, zero = jnp.bfloat16(1), jnp.bfloat16(0)
    for b in range(0, BINS, 2):
        acc = jnp.zeros((2 * nodes, 2 * half), jnp.float32)
        for r in range(0, rows, STEP):
            chunk = bins[r : r + STEP]
            mask = jnp.concatenate(
                [jnp.where(chunk <= jnp.bfloat16(b + k), one, zero) for k in range(2)], axis=1
            )
            acc += jnp.dot(sides[:, r : r + STEP], mask, preferred_element_type=jnp.float32)
        for k in range(2):
            here = acc[:, k * half : (k + 1) * half]
            out_ref[b + k] = here if before_ref is None else before_ref[b + k] + here


def choose(sizes, groups, held, feat_part, half_n, got_ref, below_ref, out_ref):
    half = below_ref.shape[2]
    nodes = below_ref.shape[1] // 2
    mine = half // feat_part
    base = lax.axis_index("core") * mine
    n_near, n_line, n_chip = sizes["near"], sizes["line"], sizes["chip"]
    n_rows = sizes["far"] * n_near
    layers = []
    for z in range(n_rows):
        cols = []
        for i in range(mine):
            chip = (base + i) // 2
            d = place_in(
                FIRST, sizes, far=z // n_near, near=z % n_near,
                line=chip // n_chip, chip=chip % n_chip, core=i % 2,
            )
            cols.append(got_ref[pl.ds(d * held, held)])
        layers += [
            jnp.concatenate([c[:, g * feat_part : (g + 1) * feat_part] for c in cols], axis=1)
            for g in range(groups)
        ]
    split = jnp.concatenate(layers, axis=0)
    left0, left1 = below_ref[0, :nodes], below_ref[0, nodes:]
    for b in range(1, BINS - 1):
        further = split >= b
        left0 = jnp.where(further, below_ref[b, :nodes], left0)
        left1 = jnp.where(further, below_ref[b, nodes:], left1)
    everything = below_ref[BINS - 1]
    eye = lax.broadcasted_iota(jnp.int32, everything.shape, 0) == lax.broadcasted_iota(
        jnp.int32, everything.shape, 1
    )
    total = jnp.sum(jnp.where(eye, everything, 0.0), axis=0, keepdims=True)
    lines = 2 * half_n + 1
    for z in range(n_rows):
        for c in range(2):
            at = (z * 2 + c) * half_n
            tile = jnp.concatenate(
                [left0[at : at + half_n], left1[at : at + half_n], total], axis=0
            )
            for line in range(n_line):
                for chip in range(n_chip):
                    d = place_in(
                        SECOND, sizes, far=z // n_near, near=z % n_near,
                        line=line, chip=chip, core=c,
                    )
                    out_ref[d * lines : (d + 1) * lines] = tile


def split_gain(half_n, node_part, sizes, part_ref, gain_ref):
    lines = 2 * half_n + 1
    after = math.prod(sizes[a] for a in SECOND[SECOND.index("core") + 1 :])
    sums = []
    for c in range(2):
        both = None
        for d in range(math.prod(sizes.values())):
            if (d // after) % 2 == c:
                one = part_ref[d * lines : (d + 1) * lines]
                both = one if both is None else both + one
        sums.append(both)
    left0 = jnp.concatenate([s[:half_n] for s in sums], axis=1)
    left1 = jnp.concatenate([s[half_n : 2 * half_n] for s in sums], axis=1)
    row = sums[0][2 * half_n :]
    where = lax.axis_index(ROWS) * node_part + lax.axis_index("core") * half_n
    lane = lax.broadcasted_iota(jnp.int32, (half_n, LANES), 1)
    at = lax.broadcasted_iota(jnp.int32, (half_n, LANES), 0) + where
    total0 = jnp.sum(jnp.where(lane == at, row, 0.0), axis=1, keepdims=True)
    total1 = jnp.sum(jnp.where(lane == at + LANES // 2, row, 0.0), axis=1, keepdims=True)
    right0 = total0 - left0
    right1 = total1 - left1
    gain_ref[...] = (
        left1 * left1 / (left0 + 1.0)
        + right1 * right1 / (right0 + 1.0)
        - total1 * total1 / (total0 + 1.0)
    ) / (total0 + 1.0)


def finish(gain_ref, theirs_ref, out_ref, best_ref):
    mine, theirs = gain_ref[...], theirs_ref[...]
    first = lax.axis_index("core") == 0
    gain = jnp.concatenate(
        [jnp.where(first, mine, theirs), jnp.where(first, theirs, mine)], axis=0
    )
    n = gain.shape[0]
    best = jnp.max(gain, axis=1, keepdims=True)
    eye = lax.broadcasted_iota(jnp.int32, (n, n), 0) == lax.broadcasted_iota(jnp.int32, (n, n), 1)
    best_ref[...] = jnp.sum(jnp.where(eye, best, 0.0), axis=0, keepdims=True)
    feats, width = gain.shape[1], out_ref.shape[1]
    own = lax.axis_index(FEAT) * width
    turned = pltpu.roll(gain, lax.rem(feats - own, feats), 1)
    out_ref[...] = turned[:, : out_ref.shape[1]]


def shards(bins, node_of, weight, label, split_bins):
    sizes = {axis: lax.axis_size(axis) for axis in ALL}
    n_rows = sizes["far"] * sizes["near"]
    n_all = math.prod(sizes.values())
    rows_here, feats = bins.shape
    node_part, feat_part = split_bins.shape
    nodes = node_part * n_rows
    half_f = feats // 2
    half_n = node_part // 2
    groups = min(LANES // feat_part, node_part)
    held = node_part // groups
    lines = 2 * half_n + 1
    pair = [(0, 1), (1, 0)]
    far_bins = lax.ppermute(bins, "core", pair)
    def k_announce(*refs):
        announce(groups, *refs)
    per_row = [x.reshape(1, rows_here) for x in (node_of, weight, label)]
    block, row, near = call(
        k_announce,
        [f32(n_all * held, LANES), f32(3, rows_here),
         jax.ShapeDtypeStruct((rows_here, half_f), jnp.int32)],
        bins, *per_row, split_bins, place=[HBM] * 5, where=[HBM, VMEM, VMEM],
        scratch=[
            pltpu.VMEM((1, rows_here), jnp.int32),
            pltpu.VMEM((1, rows_here), jnp.float32),
            pltpu.VMEM((1, rows_here), jnp.float32),
            pltpu.VMEM(split_bins.shape, jnp.int32),
            pltpu.VMEM((n_all * held, LANES), jnp.float32),
            pltpu.SemaphoreType.DMA((5 + PARTS,)),
        ],
    )
    got = lax.all_to_all(
        block.reshape(n_all, 1, held * LANES), FIRST, 0, 0, tiled=True
    ).reshape(n_all * held, LANES)
    far_row = lax.ppermute(row, "core", pair)

    def k_near(bins_ref, row_ref, out_ref):
        histogram(nodes, bins_ref, row_ref, None, out_ref)
    (below,) = call(k_near, [f32(BINS, 2 * nodes, half_f)], near, row)
    def k_far(*refs):
        histogram(nodes, *refs)
    (below,) = call(k_far, [f32(BINS, 2 * nodes, half_f)], far_bins, far_row, below)

    def k_choose(*refs):
        choose(sizes, groups, held, feat_part, half_n, *refs)
    (parts,) = call(k_choose, [f32(n_all * lines, half_f)], got, below)
    parts = lax.all_to_all(
        parts.reshape(n_all, 1, lines * half_f), SECOND, 0, 0, tiled=True
    ).reshape(n_all * lines, half_f)

    def k_gain(*refs):
        split_gain(half_n, node_part, sizes, *refs)
    (gain,) = call(k_gain, [f32(half_n, feats)], parts)
    other = lax.ppermute(gain, "core", pair)
    out, best = call(
        finish, [f32(node_part, feat_part), f32(1, node_part)], gain, other
    )
    return out, best.reshape(node_part)


def solution(mesh):
    n_rows, n_feat = mesh.devices.shape
    cores = Mesh(mesh.devices.reshape(n_rows // 2, 2, n_feat // 4, 2, 2), ALL)
    placed = (P(ALL, None), P(ALL), P(ALL), P(ALL), P(ROWS, FEAT))
    return jax.shard_map(
        shards,
        mesh=cores,
        in_specs=placed,
        out_specs=(P(ROWS, FEAT), P(ROWS)),
        check_vma=False,
    )
```

```python
import math

import jax
import jax.numpy as jnp
from jax import lax
from jax.experimental import pallas as pl
from jax.experimental.pallas import tpu as pltpu
from jax.sharding import Mesh, PartitionSpec as P

ROWS = ("far", "near")
FEAT = ("line", "chip", "core")
ALL = ROWS + FEAT
FIRST = ("core", "far", "near", "line", "chip")
SECOND = ("core", "near", "line", "chip", "far")
LANES = 128
BINS = 16
PARTS = 1
STEP = 2048
VMEM = pl.BlockSpec(memory_space=pltpu.VMEM)
HBM = pl.BlockSpec(memory_space=pltpu.HBM)
ANY = pl.BlockSpec(memory_space=pl.ANY)


def place_in(order, sizes, **at):
    d = 0
    for axis in order:
        d = d * sizes[axis] + at[axis]
    return d


def call(kernel, outs, *args, place=None, where=None, scratch=()):
    place = place or [VMEM] * len(args)
    args = [
        pltpu.with_memory_space_constraint(x, pltpu.HBM) if p is HBM else x
        for x, p in zip(args, place)
    ]
    size = sum(x.size * x.dtype.itemsize for x in (*args, *outs))
    return pl.pallas_call(
        kernel,
        out_shape=outs,
        in_specs=place,
        out_specs=tuple(where or [VMEM] * len(outs)),
        scratch_shapes=list(scratch),
        compiler_params=pltpu.CompilerParams(vmem_limit_bytes=16 << 20),
        cost_estimate=pl.CostEstimate(flops=0, bytes_accessed=size, transcendentals=0),
    )(*args)


def f32(*shape):
    return jax.ShapeDtypeStruct(shape, jnp.float32)


def bf16(*shape):
    return jax.ShapeDtypeStruct(shape, jnp.bfloat16)


def announce(groups, bins_hbm, node_hbm, weight_hbm, label_hbm, split_hbm, out_ref, row_ref,
             near_ref, node_ref, weight_ref, label_ref, split_ref, block_ref, sems):
    copies = [
        pltpu.make_async_copy(src, dst, sems.at[k])
        for k, (src, dst) in enumerate(
            ((split_hbm, split_ref), (node_hbm, node_ref), (weight_hbm, weight_ref),
             (label_hbm, label_ref))
        )
    ]
    rows, half = near_ref.shape
    part = rows // PARTS
    first = pl.multiple_of(lax.axis_index("core") * half, half)
    slabs = [
        pltpu.make_async_copy(
            bins_hbm.at[pl.ds(k * part, part), pl.ds(first, half)],
            near_ref.at[pl.ds(k * part, part)],
            sems.at[5 + k],
        )
        for k in range(PARTS)
    ]
    for c in copies + slabs:
        c.start()
    copies[0].wait()
    split = split_ref[...].astype(jnp.float32)
    held = split.shape[0] // groups
    block = jnp.concatenate(
        [split[g * held : (g + 1) * held] for g in range(groups)], axis=1
    )
    if block.shape[1] < LANES:
        block = jnp.concatenate(
            [block, jnp.zeros((held, LANES - block.shape[1]), jnp.float32)], axis=1
        )
    many = max(1, 8 // held)
    some = jnp.concatenate([block] * many, axis=0)
    for k in range(block_ref.shape[0] // some.shape[0]):
        block_ref[k * some.shape[0] : (k + 1) * some.shape[0]] = some
    out = pltpu.make_async_copy(block_ref, out_ref, sems.at[4])
    out.start()
    for c in copies[1:]:
        c.wait()
    weight = weight_ref[...]
    row_ref[0:1] = node_ref[...].astype(jnp.float32)
    row_ref[1:2] = weight.astype(jnp.bfloat16).astype(jnp.float32)
    row_ref[2:3] = (weight * label_ref[...]).astype(jnp.bfloat16).astype(jnp.float32)
    for c in slabs:
        c.wait()
    out.wait()


def sides_of(nodes, row_ref):
    node = row_ref[0:1].astype(jnp.int32)
    hot = lax.broadcasted_iota(jnp.int32, (nodes, node.shape[1]), 0) == node
    return jnp.concatenate(
        [jnp.where(hot, row_ref[1:2], 0.0), jnp.where(hot, row_ref[2:3], 0.0)], axis=0
    ).astype(jnp.bfloat16)


def histogram(nodes, bins_ref, row_ref, before_ref, out_ref):
    half = out_ref.shape[2]
    rows, width = bins_ref.shape
    if width == half:
        bins = bins_ref[...]
    else:
        first = pl.multiple_of(lax.axis_index("core") * half, half)
        bins = bins_ref[:, pl.ds(first, half)]
    bins = bins.astype(jnp.bfloat16)
    sides = sides_of(nodes, row_ref)
    one, zero = jnp.bfloat16(1), jnp.bfloat16(0)
    for b in range(0, BINS, 2):
        acc = jnp.zeros((2 * nodes, 2 * half), jnp.float32)
        for r in range(0, rows, STEP):
            chunk = bins[r : r + STEP]
            mask = jnp.concatenate(
                [jnp.where(chunk <= jnp.bfloat16(b + k), one, zero) for k in range(2)], axis=1
            )
            acc += jnp.dot(sides[:, r : r + STEP], mask, preferred_element_type=jnp.float32)
        for k in range(2):
            here = acc[:, k * half : (k + 1) * half]
            out_ref[b + k] = here if before_ref is None else before_ref[b + k] + here


def choose(sizes, groups, held, feat_part, half_n, got_ref, below_ref, out_ref):
    half = below_ref.shape[2]
    nodes = below_ref.shape[1] // 2
    mine = half // feat_part
    base = lax.axis_index("core") * mine
    n_near, n_line, n_chip = sizes["near"], sizes["line"], sizes["chip"]
    n_rows = sizes["far"] * n_near
    layers = []
    for z in range(n_rows):
        cols = []
        for i in range(mine):
            chip = (base + i) // 2
            d = place_in(
                FIRST, sizes, far=z // n_near, near=z % n_near,
                line=chip // n_chip, chip=chip % n_chip, core=i % 2,
            )
            cols.append(got_ref[pl.ds(d * held, held)])
        layers += [
            jnp.concatenate([c[:, g * feat_part : (g + 1) * feat_part] for c in cols], axis=1)
            for g in range(groups)
        ]
    split = jnp.concatenate(layers, axis=0)
    left0, left1 = below_ref[0, :nodes], below_ref[0, nodes:]
    for b in range(1, BINS - 1):
        further = split >= b
        left0 = jnp.where(further, below_ref[b, :nodes], left0)
        left1 = jnp.where(further, below_ref[b, nodes:], left1)
    everything = below_ref[BINS - 1]
    eye = lax.broadcasted_iota(jnp.int32, everything.shape, 0) == lax.broadcasted_iota(
        jnp.int32, everything.shape, 1
    )
    total = jnp.sum(jnp.where(eye, everything, 0.0), axis=0, keepdims=True)
    lines = 2 * half_n + 1
    for z in range(n_rows):
        for c in range(2):
            at = (z * 2 + c) * half_n
            tile = jnp.concatenate(
                [left0[at : at + half_n], left1[at : at + half_n], total], axis=0
            )
            for line in range(n_line):
                for chip in range(n_chip):
                    d = place_in(
                        SECOND, sizes, far=z // n_near, near=z % n_near,
                        line=line, chip=chip, core=c,
                    )
                    out_ref[d * lines : (d + 1) * lines] = tile


def split_gain(half_n, node_part, sizes, part_ref, gain_ref):
    lines = 2 * half_n + 1
    after = math.prod(sizes[a] for a in SECOND[SECOND.index("core") + 1 :])
    sums = []
    for c in range(2):
        both = None
        for d in range(math.prod(sizes.values())):
            if (d // after) % 2 == c:
                one = part_ref[d * lines : (d + 1) * lines]
                both = one if both is None else both + one
        sums.append(both)
    left0 = jnp.concatenate([s[:half_n] for s in sums], axis=1)
    left1 = jnp.concatenate([s[half_n : 2 * half_n] for s in sums], axis=1)
    row = sums[0][2 * half_n :]
    where = lax.axis_index(ROWS) * node_part + lax.axis_index("core") * half_n
    lane = lax.broadcasted_iota(jnp.int32, (half_n, LANES), 1)
    at = lax.broadcasted_iota(jnp.int32, (half_n, LANES), 0) + where
    total0 = jnp.sum(jnp.where(lane == at, row, 0.0), axis=1, keepdims=True)
    total1 = jnp.sum(jnp.where(lane == at + LANES // 2, row, 0.0), axis=1, keepdims=True)
    right0 = total0 - left0
    right1 = total1 - left1
    gain_ref[...] = (
        left1 * left1 / (left0 + 1.0)
        + right1 * right1 / (right0 + 1.0)
        - total1 * total1 / (total0 + 1.0)
    ) / (total0 + 1.0)


def finish(gain_ref, theirs_ref, out_ref, best_ref):
    mine, theirs = gain_ref[...], theirs_ref[...]
    first = lax.axis_index("core") == 0
    gain = jnp.concatenate(
        [jnp.where(first, mine, theirs), jnp.where(first, theirs, mine)], axis=0
    )
    n = gain.shape[0]
    best = jnp.max(gain, axis=1, keepdims=True)
    eye = lax.broadcasted_iota(jnp.int32, (n, n), 0) == lax.broadcasted_iota(jnp.int32, (n, n), 1)
    best_ref[...] = jnp.sum(jnp.where(eye, best, 0.0), axis=0, keepdims=True)
    feats, width = gain.shape[1], out_ref.shape[1]
    own = lax.axis_index(FEAT) * width
    turned = pltpu.roll(gain, lax.rem(feats - own, feats), 1)
    out_ref[...] = turned[:, : out_ref.shape[1]]


def shards(bins, node_of, weight, label, split_bins):
    sizes = {axis: lax.axis_size(axis) for axis in ALL}
    n_rows = sizes["far"] * sizes["near"]
    n_all = math.prod(sizes.values())
    rows_here, feats = bins.shape
    node_part, feat_part = split_bins.shape
    nodes = node_part * n_rows
    half_f = feats // 2
    half_n = node_part // 2
    groups = min(LANES // feat_part, node_part)
    held = node_part // groups
    lines = 2 * half_n + 1
    pair = [(0, 1), (1, 0)]
    far_bins = lax.ppermute(bins, "core", pair)
    def k_announce(*refs):
        announce(groups, *refs)
    per_row = [x.reshape(1, rows_here) for x in (node_of, weight, label)]
    block, row, near = call(
        k_announce,
        [f32(n_all * held, LANES), f32(3, rows_here),
         jax.ShapeDtypeStruct((rows_here, half_f), jnp.int32)],
        bins, *per_row, split_bins, place=[HBM] * 5, where=[HBM, VMEM, VMEM],
        scratch=[
            pltpu.VMEM((1, rows_here), jnp.int32),
            pltpu.VMEM((1, rows_here), jnp.float32),
            pltpu.VMEM((1, rows_here), jnp.float32),
            pltpu.VMEM(split_bins.shape, jnp.int32),
            pltpu.VMEM((n_all * held, LANES), jnp.float32),
            pltpu.SemaphoreType.DMA((5 + PARTS,)),
        ],
    )
    got = lax.all_to_all(
        block.reshape(n_all, 1, held * LANES), FIRST, 0, 0, tiled=True
    ).reshape(n_all * held, LANES)
    far_row = lax.ppermute(row, "core", pair)

    def k_near(bins_ref, row_ref, out_ref):
        histogram(nodes, bins_ref, row_ref, None, out_ref)
    (below,) = call(k_near, [f32(BINS, 2 * nodes, half_f)], near, row)
    def k_far(*refs):
        histogram(nodes, *refs)
    (below,) = call(k_far, [f32(BINS, 2 * nodes, half_f)], far_bins, far_row, below)

    def k_choose(*refs):
        choose(sizes, groups, held, feat_part, half_n, *refs)
    (parts,) = call(k_choose, [f32(n_all * lines, half_f)], got, below)
    parts = lax.all_to_all(
        parts.reshape(n_all, 1, lines * half_f), SECOND, 0, 0, tiled=True
    ).reshape(n_all * lines, half_f)

    def k_gain(*refs):
        split_gain(half_n, node_part, sizes, *refs)
    (gain,) = call(k_gain, [f32(half_n, feats)], parts)
    other = lax.ppermute(gain, "core", pair)
    out, best = call(
        finish, [f32(node_part, feat_part), f32(1, node_part)], gain, other
    )
    return out, best.reshape(node_part)


def solution(mesh):
    n_rows, n_feat = mesh.devices.shape
    cores = Mesh(mesh.devices.reshape(n_rows // 2, 2, n_feat // 4, 2, 2), ALL)
    placed = (P(ALL, None), P(ALL), P(ALL), P(ALL), P(ROWS, FEAT))
    return jax.shard_map(
        shards,
        mesh=cores,
        in_specs=placed,
        out_specs=(P(ROWS, FEAT), P(ROWS)),
        check_vma=False,
    )
```

```python
import math

import jax
import jax.numpy as jnp
from jax import lax
from jax.experimental import pallas as pl
from jax.experimental.pallas import tpu as pltpu
from jax.sharding import Mesh, PartitionSpec as P

ROWS = ("far", "near")
FEAT = ("line", "chip", "core")
ALL = ROWS + FEAT
FIRST = ("near", "core", "far", "line", "chip")
SECOND = ("core", "near", "line", "chip", "far")
LANES = 128
BINS = 16
PARTS = 1
STEP = 2048
VMEM = pl.BlockSpec(memory_space=pltpu.VMEM)
HBM = pl.BlockSpec(memory_space=pltpu.HBM)
ANY = pl.BlockSpec(memory_space=pl.ANY)


def place_in(order, sizes, **at):
    d = 0
    for axis in order:
        d = d * sizes[axis] + at[axis]
    return d


def call(kernel, outs, *args, place=None, where=None, scratch=()):
    place = place or [VMEM] * len(args)
    args = [
        pltpu.with_memory_space_constraint(x, pltpu.HBM) if p is HBM else x
        for x, p in zip(args, place)
    ]
    size = sum(x.size * x.dtype.itemsize for x in (*args, *outs))
    return pl.pallas_call(
        kernel,
        out_shape=outs,
        in_specs=place,
        out_specs=tuple(where or [VMEM] * len(outs)),
        scratch_shapes=list(scratch),
        compiler_params=pltpu.CompilerParams(vmem_limit_bytes=16 << 20),
        cost_estimate=pl.CostEstimate(flops=0, bytes_accessed=size, transcendentals=0),
    )(*args)


def f32(*shape):
    return jax.ShapeDtypeStruct(shape, jnp.float32)


def bf16(*shape):
    return jax.ShapeDtypeStruct(shape, jnp.bfloat16)


def announce(groups, bins_hbm, node_hbm, weight_hbm, label_hbm, split_hbm, out_ref, row_ref,
             near_ref, node_ref, weight_ref, label_ref, split_ref, block_ref, sems):
    copies = [
        pltpu.make_async_copy(src, dst, sems.at[k])
        for k, (src, dst) in enumerate(
            ((split_hbm, split_ref), (node_hbm, node_ref), (weight_hbm, weight_ref),
             (label_hbm, label_ref))
        )
    ]
    rows, half = near_ref.shape
    part = rows // PARTS
    first = pl.multiple_of(lax.axis_index("core") * half, half)
    slabs = [
        pltpu.make_async_copy(
            bins_hbm.at[pl.ds(k * part, part), pl.ds(first, half)],
            near_ref.at[pl.ds(k * part, part)],
            sems.at[5 + k],
        )
        for k in range(PARTS)
    ]
    for c in copies + slabs:
        c.start()
    copies[0].wait()
    split = split_ref[...].astype(jnp.float32)
    held = split.shape[0] // groups
    block = jnp.concatenate(
        [split[g * held : (g + 1) * held] for g in range(groups)], axis=1
    )
    if block.shape[1] < LANES:
        block = jnp.concatenate(
            [block, jnp.zeros((held, LANES - block.shape[1]), jnp.float32)], axis=1
        )
    many = max(1, 8 // held)
    some = jnp.concatenate([block] * many, axis=0)
    for k in range(block_ref.shape[0] // some.shape[0]):
        block_ref[k * some.shape[0] : (k + 1) * some.shape[0]] = some
    out = pltpu.make_async_copy(block_ref, out_ref, sems.at[4])
    out.start()
    for c in copies[1:]:
        c.wait()
    weight = weight_ref[...]
    row_ref[0:1] = node_ref[...].astype(jnp.float32)
    row_ref[1:2] = weight.astype(jnp.bfloat16).astype(jnp.float32)
    row_ref[2:3] = (weight * label_ref[...]).astype(jnp.bfloat16).astype(jnp.float32)
    for c in slabs:
        c.wait()
    out.wait()


def sides_of(nodes, row_ref):
    node = row_ref[0:1].astype(jnp.int32)
    hot = lax.broadcasted_iota(jnp.int32, (nodes, node.shape[1]), 0) == node
    return jnp.concatenate(
        [jnp.where(hot, row_ref[1:2], 0.0), jnp.where(hot, row_ref[2:3], 0.0)], axis=0
    ).astype(jnp.bfloat16)


def histogram(nodes, bins_ref, row_ref, before_ref, out_ref):
    half = out_ref.shape[2]
    rows, width = bins_ref.shape
    if width == half:
        bins = bins_ref[...]
    else:
        first = pl.multiple_of(lax.axis_index("core") * half, half)
        bins = bins_ref[:, pl.ds(first, half)]
    bins = bins.astype(jnp.bfloat16)
    sides = sides_of(nodes, row_ref)
    one, zero = jnp.bfloat16(1), jnp.bfloat16(0)
    for b in range(0, BINS, 2):
        acc = jnp.zeros((2 * nodes, 2 * half), jnp.float32)
        for r in range(0, rows, STEP):
            chunk = bins[r : r + STEP]
            mask = jnp.concatenate(
                [jnp.where(chunk <= jnp.bfloat16(b + k), one, zero) for k in range(2)], axis=1
            )
            acc += jnp.dot(sides[:, r : r + STEP], mask, preferred_element_type=jnp.float32)
        for k in range(2):
            here = acc[:, k * half : (k + 1) * half]
            out_ref[b + k] = here if before_ref is None else before_ref[b + k] + here


def choose(sizes, groups, held, feat_part, half_n, got_ref, below_ref, out_ref):
    half = below_ref.shape[2]
    nodes = below_ref.shape[1] // 2
    mine = half // feat_part
    base = lax.axis_index("core") * mine
    n_near, n_line, n_chip = sizes["near"], sizes["line"], sizes["chip"]
    n_rows = sizes["far"] * n_near
    layers = []
    for z in range(n_rows):
        cols = []
        for i in range(mine):
            chip = (base + i) // 2
            d = place_in(
                FIRST, sizes, far=z // n_near, near=z % n_near,
                line=chip // n_chip, chip=chip % n_chip, core=i % 2,
            )
            cols.append(got_ref[pl.ds(d * held, held)])
        layers += [
            jnp.concatenate([c[:, g * feat_part : (g + 1) * feat_part] for c in cols], axis=1)
            for g in range(groups)
        ]
    split = jnp.concatenate(layers, axis=0)
    left0, left1 = below_ref[0, :nodes], below_ref[0, nodes:]
    for b in range(1, BINS - 1):
        further = split >= b
        left0 = jnp.where(further, below_ref[b, :nodes], left0)
        left1 = jnp.where(further, below_ref[b, nodes:], left1)
    everything = below_ref[BINS - 1]
    eye = lax.broadcasted_iota(jnp.int32, everything.shape, 0) == lax.broadcasted_iota(
        jnp.int32, everything.shape, 1
    )
    total = jnp.sum(jnp.where(eye, everything, 0.0), axis=0, keepdims=True)
    lines = 2 * half_n + 1
    for z in range(n_rows):
        for c in range(2):
            at = (z * 2 + c) * half_n
            tile = jnp.concatenate(
                [left0[at : at + half_n], left1[at : at + half_n], total], axis=0
            )
            for line in range(n_line):
                for chip in range(n_chip):
                    d = place_in(
                        SECOND, sizes, far=z // n_near, near=z % n_near,
                        line=line, chip=chip, core=c,
                    )
                    out_ref[d * lines : (d + 1) * lines] = tile


def split_gain(half_n, node_part, sizes, part_ref, gain_ref):
    lines = 2 * half_n + 1
    after = math.prod(sizes[a] for a in SECOND[SECOND.index("core") + 1 :])
    sums = []
    for c in range(2):
        both = None
        for d in range(math.prod(sizes.values())):
            if (d // after) % 2 == c:
                one = part_ref[d * lines : (d + 1) * lines]
                both = one if both is None else both + one
        sums.append(both)
    left0 = jnp.concatenate([s[:half_n] for s in sums], axis=1)
    left1 = jnp.concatenate([s[half_n : 2 * half_n] for s in sums], axis=1)
    row = sums[0][2 * half_n :]
    where = lax.axis_index(ROWS) * node_part + lax.axis_index("core") * half_n
    lane = lax.broadcasted_iota(jnp.int32, (half_n, LANES), 1)
    at = lax.broadcasted_iota(jnp.int32, (half_n, LANES), 0) + where
    total0 = jnp.sum(jnp.where(lane == at, row, 0.0), axis=1, keepdims=True)
    total1 = jnp.sum(jnp.where(lane == at + LANES // 2, row, 0.0), axis=1, keepdims=True)
    right0 = total0 - left0
    right1 = total1 - left1
    gain_ref[...] = (
        left1 * left1 / (left0 + 1.0)
        + right1 * right1 / (right0 + 1.0)
        - total1 * total1 / (total0 + 1.0)
    ) / (total0 + 1.0)


def finish(gain_ref, theirs_ref, out_ref, best_ref):
    mine, theirs = gain_ref[...], theirs_ref[...]
    first = lax.axis_index("core") == 0
    gain = jnp.concatenate(
        [jnp.where(first, mine, theirs), jnp.where(first, theirs, mine)], axis=0
    )
    n = gain.shape[0]
    best = jnp.max(gain, axis=1, keepdims=True)
    eye = lax.broadcasted_iota(jnp.int32, (n, n), 0) == lax.broadcasted_iota(jnp.int32, (n, n), 1)
    best_ref[...] = jnp.sum(jnp.where(eye, best, 0.0), axis=0, keepdims=True)
    feats, width = gain.shape[1], out_ref.shape[1]
    own = lax.axis_index(FEAT) * width
    turned = pltpu.roll(gain, lax.rem(feats - own, feats), 1)
    out_ref[...] = turned[:, : out_ref.shape[1]]


def shards(bins, node_of, weight, label, split_bins):
    sizes = {axis: lax.axis_size(axis) for axis in ALL}
    n_rows = sizes["far"] * sizes["near"]
    n_all = math.prod(sizes.values())
    rows_here, feats = bins.shape
    node_part, feat_part = split_bins.shape
    nodes = node_part * n_rows
    half_f = feats // 2
    half_n = node_part // 2
    groups = min(LANES // feat_part, node_part)
    held = node_part // groups
    lines = 2 * half_n + 1
    pair = [(0, 1), (1, 0)]
    far_bins = lax.ppermute(bins, "core", pair)
    def k_announce(*refs):
        announce(groups, *refs)
    per_row = [x.reshape(1, rows_here) for x in (node_of, weight, label)]
    block, row, near = call(
        k_announce,
        [f32(n_all * held, LANES), f32(3, rows_here),
         jax.ShapeDtypeStruct((rows_here, half_f), jnp.int32)],
        bins, *per_row, split_bins, place=[HBM] * 5, where=[HBM, VMEM, VMEM],
        scratch=[
            pltpu.VMEM((1, rows_here), jnp.int32),
            pltpu.VMEM((1, rows_here), jnp.float32),
            pltpu.VMEM((1, rows_here), jnp.float32),
            pltpu.VMEM(split_bins.shape, jnp.int32),
            pltpu.VMEM((n_all * held, LANES), jnp.float32),
            pltpu.SemaphoreType.DMA((5 + PARTS,)),
        ],
    )
    got = lax.all_to_all(
        block.reshape(n_all, 1, held * LANES), FIRST, 0, 0, tiled=True
    ).reshape(n_all * held, LANES)
    far_row = lax.ppermute(row, "core", pair)

    def k_near(bins_ref, row_ref, out_ref):
        histogram(nodes, bins_ref, row_ref, None, out_ref)
    (below,) = call(k_near, [f32(BINS, 2 * nodes, half_f)], near, row)
    def k_far(*refs):
        histogram(nodes, *refs)
    (below,) = call(k_far, [f32(BINS, 2 * nodes, half_f)], far_bins, far_row, below)

    def k_choose(*refs):
        choose(sizes, groups, held, feat_part, half_n, *refs)
    (parts,) = call(k_choose, [f32(n_all * lines, half_f)], got, below)
    parts = lax.all_to_all(
        parts.reshape(n_all, 1, lines * half_f), SECOND, 0, 0, tiled=True
    ).reshape(n_all * lines, half_f)

    def k_gain(*refs):
        split_gain(half_n, node_part, sizes, *refs)
    (gain,) = call(k_gain, [f32(half_n, feats)], parts)
    other = lax.ppermute(gain, "core", pair)
    out, best = call(
        finish, [f32(node_part, feat_part), f32(1, node_part)], gain, other
    )
    return out, best.reshape(node_part)


def solution(mesh):
    n_rows, n_feat = mesh.devices.shape
    cores = Mesh(mesh.devices.reshape(n_rows // 2, 2, n_feat // 4, 2, 2), ALL)
    placed = (P(ALL, None), P(ALL), P(ALL), P(ALL), P(ROWS, FEAT))
    return jax.shard_map(
        shards,
        mesh=cores,
        in_specs=placed,
        out_specs=(P(ROWS, FEAT), P(ROWS)),
        check_vma=False,
    )
```

```python
import math

import jax
import jax.numpy as jnp
from jax import lax
from jax.experimental import pallas as pl
from jax.experimental.pallas import tpu as pltpu
from jax.sharding import Mesh, PartitionSpec as P

ROWS = ("far", "near")
FEAT = ("line", "chip", "core")
ALL = ROWS + FEAT
FIRST = ("near", "core", "far", "line", "chip")
SECOND = ("core", "near", "line", "chip", "far")
LANES = 128
BINS = 16
PARTS = 1
STEP = 2048
VMEM = pl.BlockSpec(memory_space=pltpu.VMEM)
HBM = pl.BlockSpec(memory_space=pltpu.HBM)
ANY = pl.BlockSpec(memory_space=pl.ANY)


def place_in(order, sizes, **at):
    d = 0
    for axis in order:
        d = d * sizes[axis] + at[axis]
    return d


def call(kernel, outs, *args, place=None, where=None, scratch=()):
    place = place or [VMEM] * len(args)
    args = [
        pltpu.with_memory_space_constraint(x, pltpu.HBM) if p is HBM else x
        for x, p in zip(args, place)
    ]
    size = sum(x.size * x.dtype.itemsize for x in (*args, *outs))
    return pl.pallas_call(
        kernel,
        out_shape=outs,
        in_specs=place,
        out_specs=tuple(where or [VMEM] * len(outs)),
        scratch_shapes=list(scratch),
        compiler_params=pltpu.CompilerParams(vmem_limit_bytes=16 << 20),
        cost_estimate=pl.CostEstimate(flops=0, bytes_accessed=size, transcendentals=0),
    )(*args)


def f32(*shape):
    return jax.ShapeDtypeStruct(shape, jnp.float32)


def bf16(*shape):
    return jax.ShapeDtypeStruct(shape, jnp.bfloat16)


def announce(groups, bins_hbm, node_hbm, weight_hbm, label_hbm, split_hbm, out_ref, row_ref,
             near_ref, node_ref, weight_ref, label_ref, split_ref, block_ref, sems):
    copies = [
        pltpu.make_async_copy(src, dst, sems.at[k])
        for k, (src, dst) in enumerate(
            ((split_hbm, split_ref), (node_hbm, node_ref), (weight_hbm, weight_ref),
             (label_hbm, label_ref))
        )
    ]
    rows, half = near_ref.shape
    part = rows // PARTS
    first = pl.multiple_of(lax.axis_index("core") * half, half)
    slabs = [
        pltpu.make_async_copy(
            bins_hbm.at[pl.ds(k * part, part), pl.ds(first, half)],
            near_ref.at[pl.ds(k * part, part)],
            sems.at[5 + k],
        )
        for k in range(PARTS)
    ]
    for c in copies + slabs:
        c.start()
    copies[0].wait()
    split = split_ref[...].astype(jnp.float32)
    held = split.shape[0] // groups
    block = jnp.concatenate(
        [split[g * held : (g + 1) * held] for g in range(groups)], axis=1
    )
    if block.shape[1] < LANES:
        block = jnp.concatenate(
            [block, jnp.zeros((held, LANES - block.shape[1]), jnp.float32)], axis=1
        )
    many = max(1, 8 // held)
    some = jnp.concatenate([block] * many, axis=0)
    for k in range(block_ref.shape[0] // some.shape[0]):
        block_ref[k * some.shape[0] : (k + 1) * some.shape[0]] = some
    out = pltpu.make_async_copy(block_ref, out_ref, sems.at[4])
    out.start()
    for c in copies[1:]:
        c.wait()
    weight = weight_ref[...]
    row_ref[0:1] = node_ref[...].astype(jnp.float32)
    row_ref[1:2] = weight.astype(jnp.bfloat16).astype(jnp.float32)
    row_ref[2:3] = (weight * label_ref[...]).astype(jnp.bfloat16).astype(jnp.float32)
    for c in slabs:
        c.wait()
    out.wait()


def sides_of(nodes, row_ref):
    node = row_ref[0:1].astype(jnp.int32)
    hot = lax.broadcasted_iota(jnp.int32, (nodes, node.shape[1]), 0) == node
    return jnp.concatenate(
        [jnp.where(hot, row_ref[1:2], 0.0), jnp.where(hot, row_ref[2:3], 0.0)], axis=0
    ).astype(jnp.bfloat16)


def histogram(nodes, bins_ref, row_ref, before_ref, out_ref):
    half = out_ref.shape[2]
    rows, width = bins_ref.shape
    if width == half:
        bins = bins_ref[...]
    else:
        first = pl.multiple_of(lax.axis_index("core") * half, half)
        bins = bins_ref[:, pl.ds(first, half)]
    bins = bins.astype(jnp.bfloat16)
    sides = sides_of(nodes, row_ref)
    one, zero = jnp.bfloat16(1), jnp.bfloat16(0)
    for b in range(0, BINS, 2):
        acc = jnp.zeros((2 * nodes, 2 * half), jnp.float32)
        for r in range(0, rows, STEP):
            chunk = bins[r : r + STEP]
            mask = jnp.concatenate(
                [jnp.where(chunk <= jnp.bfloat16(b + k), one, zero) for k in range(2)], axis=1
            )
            acc += jnp.dot(sides[:, r : r + STEP], mask, preferred_element_type=jnp.float32)
        for k in range(2):
            here = acc[:, k * half : (k + 1) * half]
            out_ref[b + k] = here if before_ref is None else before_ref[b + k] + here


def choose(sizes, groups, held, feat_part, half_n, got_ref, below_ref, out_ref):
    half = below_ref.shape[2]
    nodes = below_ref.shape[1] // 2
    mine = half // feat_part
    base = lax.axis_index("core") * mine
    n_near, n_line, n_chip = sizes["near"], sizes["line"], sizes["chip"]
    n_rows = sizes["far"] * n_near
    layers = []
    for z in range(n_rows):
        cols = []
        for i in range(mine):
            chip = (base + i) // 2
            d = place_in(
                FIRST, sizes, far=z // n_near, near=z % n_near,
                line=chip // n_chip, chip=chip % n_chip, core=i % 2,
            )
            cols.append(got_ref[pl.ds(d * held, held)])
        layers += [
            jnp.concatenate([c[:, g * feat_part : (g + 1) * feat_part] for c in cols], axis=1)
            for g in range(groups)
        ]
    split = jnp.concatenate(layers, axis=0)
    left0, left1 = below_ref[0, :nodes], below_ref[0, nodes:]
    for b in range(1, BINS - 1):
        further = split >= b
        left0 = jnp.where(further, below_ref[b, :nodes], left0)
        left1 = jnp.where(further, below_ref[b, nodes:], left1)
    everything = below_ref[BINS - 1]
    eye = lax.broadcasted_iota(jnp.int32, everything.shape, 0) == lax.broadcasted_iota(
        jnp.int32, everything.shape, 1
    )
    total = jnp.sum(jnp.where(eye, everything, 0.0), axis=0, keepdims=True)
    lines = 2 * half_n + 1
    for z in range(n_rows):
        for c in range(2):
            at = (z * 2 + c) * half_n
            tile = jnp.concatenate(
                [left0[at : at + half_n], left1[at : at + half_n], total], axis=0
            )
            for line in range(n_line):
                for chip in range(n_chip):
                    d = place_in(
                        SECOND, sizes, far=z // n_near, near=z % n_near,
                        line=line, chip=chip, core=c,
                    )
                    out_ref[d * lines : (d + 1) * lines] = tile


def split_gain(half_n, node_part, sizes, part_ref, gain_ref):
    lines = 2 * half_n + 1
    after = math.prod(sizes[a] for a in SECOND[SECOND.index("core") + 1 :])
    sums = []
    for c in range(2):
        both = None
        for d in range(math.prod(sizes.values())):
            if (d // after) % 2 == c:
                one = part_ref[d * lines : (d + 1) * lines]
                both = one if both is None else both + one
        sums.append(both)
    left0 = jnp.concatenate([s[:half_n] for s in sums], axis=1)
    left1 = jnp.concatenate([s[half_n : 2 * half_n] for s in sums], axis=1)
    row = sums[0][2 * half_n :]
    where = lax.axis_index(ROWS) * node_part + lax.axis_index("core") * half_n
    lane = lax.broadcasted_iota(jnp.int32, (half_n, LANES), 1)
    at = lax.broadcasted_iota(jnp.int32, (half_n, LANES), 0) + where
    total0 = jnp.sum(jnp.where(lane == at, row, 0.0), axis=1, keepdims=True)
    total1 = jnp.sum(jnp.where(lane == at + LANES // 2, row, 0.0), axis=1, keepdims=True)
    right0 = total0 - left0
    right1 = total1 - left1
    gain_ref[...] = (
        left1 * left1 / (left0 + 1.0)
        + right1 * right1 / (right0 + 1.0)
        - total1 * total1 / (total0 + 1.0)
    ) / (total0 + 1.0)


def finish(gain_ref, theirs_ref, out_hbm, best_hbm, out_ref, best_ref, sems):
    mine, theirs = gain_ref[...], theirs_ref[...]
    first = lax.axis_index("core") == 0
    gain = jnp.concatenate(
        [jnp.where(first, mine, theirs), jnp.where(first, theirs, mine)], axis=0
    )
    feats, width = gain.shape[1], out_ref.shape[1]
    own = lax.axis_index(FEAT) * width
    turned = pltpu.roll(gain, lax.rem(feats - own, feats), 1)
    out_ref[...] = turned[:, : out_ref.shape[1]]
    gain_out = pltpu.make_async_copy(out_ref, out_hbm, sems.at[0])
    gain_out.start()
    n = gain.shape[0]
    best = jnp.max(gain, axis=1, keepdims=True)
    eye = lax.broadcasted_iota(jnp.int32, (n, n), 0) == lax.broadcasted_iota(jnp.int32, (n, n), 1)
    best_ref[...] = jnp.sum(jnp.where(eye, best, 0.0), axis=0, keepdims=True)
    best_out = pltpu.make_async_copy(best_ref, best_hbm, sems.at[1])
    best_out.start()
    gain_out.wait()
    best_out.wait()


def shards(bins, node_of, weight, label, split_bins):
    sizes = {axis: lax.axis_size(axis) for axis in ALL}
    n_rows = sizes["far"] * sizes["near"]
    n_all = math.prod(sizes.values())
    rows_here, feats = bins.shape
    node_part, feat_part = split_bins.shape
    nodes = node_part * n_rows
    half_f = feats // 2
    half_n = node_part // 2
    groups = min(LANES // feat_part, node_part)
    held = node_part // groups
    lines = 2 * half_n + 1
    pair = [(0, 1), (1, 0)]
    far_bins = lax.ppermute(bins, "core", pair)
    def k_announce(*refs):
        announce(groups, *refs)
    per_row = [x.reshape(1, rows_here) for x in (node_of, weight, label)]
    block, row, near = call(
        k_announce,
        [f32(n_all * held, LANES), f32(3, rows_here),
         jax.ShapeDtypeStruct((rows_here, half_f), jnp.int32)],
        bins, *per_row, split_bins, place=[HBM] * 5, where=[HBM, VMEM, VMEM],
        scratch=[
            pltpu.VMEM((1, rows_here), jnp.int32),
            pltpu.VMEM((1, rows_here), jnp.float32),
            pltpu.VMEM((1, rows_here), jnp.float32),
            pltpu.VMEM(split_bins.shape, jnp.int32),
            pltpu.VMEM((n_all * held, LANES), jnp.float32),
            pltpu.SemaphoreType.DMA((5 + PARTS,)),
        ],
    )
    got = lax.all_to_all(
        block.reshape(n_all, 1, held * LANES), FIRST, 0, 0, tiled=True
    ).reshape(n_all * held, LANES)
    far_row = lax.ppermute(row, "core", pair)

    def k_near(bins_ref, row_ref, out_ref):
        histogram(nodes, bins_ref, row_ref, None, out_ref)
    (below,) = call(k_near, [f32(BINS, 2 * nodes, half_f)], near, row)
    def k_far(*refs):
        histogram(nodes, *refs)
    (below,) = call(k_far, [f32(BINS, 2 * nodes, half_f)], far_bins, far_row, below)

    def k_choose(*refs):
        choose(sizes, groups, held, feat_part, half_n, *refs)
    (parts,) = call(k_choose, [f32(n_all * lines, half_f)], got, below)
    parts = lax.all_to_all(
        parts.reshape(n_all, 1, lines * half_f), SECOND, 0, 0, tiled=True
    ).reshape(n_all * lines, half_f)

    def k_gain(*refs):
        split_gain(half_n, node_part, sizes, *refs)
    (gain,) = call(k_gain, [f32(half_n, feats)], parts)
    other = lax.ppermute(gain, "core", pair)
    out, best = call(
        finish, [f32(node_part, feat_part), f32(1, node_part)], gain, other,
        where=[HBM, HBM],
        scratch=[
            pltpu.VMEM((node_part, feat_part), jnp.float32),
            pltpu.VMEM((1, node_part), jnp.float32),
            pltpu.SemaphoreType.DMA((2,)),
        ],
    )
    return out, best.reshape(node_part)


def solution(mesh):
    n_rows, n_feat = mesh.devices.shape
    cores = Mesh(mesh.devices.reshape(n_rows // 2, 2, n_feat // 4, 2, 2), ALL)
    placed = (P(ALL, None), P(ALL), P(ALL), P(ALL), P(ROWS, FEAT))
    return jax.shard_map(
        shards,
        mesh=cores,
        in_specs=placed,
        out_specs=(P(ROWS, FEAT), P(ROWS)),
        check_vma=False,
    )
```

```python
import math

import jax
import jax.numpy as jnp
from jax import lax
from jax.experimental import pallas as pl
from jax.experimental.pallas import tpu as pltpu
from jax.sharding import Mesh, PartitionSpec as P

ROWS = ("far", "near")
FEAT = ("line", "chip", "core")
ALL = ROWS + FEAT
FIRST = ("near", "core", "far", "line", "chip")
SECOND = ("core", "near", "line", "chip", "far")
LANES = 128
BINS = 16
PARTS = 1
STEP = 2048
VMEM = pl.BlockSpec(memory_space=pltpu.VMEM)
HBM = pl.BlockSpec(memory_space=pltpu.HBM)
ANY = pl.BlockSpec(memory_space=pl.ANY)


def place_in(order, sizes, **at):
    d = 0
    for axis in order:
        d = d * sizes[axis] + at[axis]
    return d


def call(kernel, outs, *args, place=None, where=None, scratch=()):
    place = place or [VMEM] * len(args)
    args = [
        pltpu.with_memory_space_constraint(x, pltpu.HBM) if p is HBM else x
        for x, p in zip(args, place)
    ]
    size = sum(x.size * x.dtype.itemsize for x in (*args, *outs))
    return pl.pallas_call(
        kernel,
        out_shape=outs,
        in_specs=place,
        out_specs=tuple(where or [VMEM] * len(outs)),
        scratch_shapes=list(scratch),
        compiler_params=pltpu.CompilerParams(vmem_limit_bytes=16 << 20),
        cost_estimate=pl.CostEstimate(flops=0, bytes_accessed=size, transcendentals=0),
    )(*args)


def f32(*shape):
    return jax.ShapeDtypeStruct(shape, jnp.float32)


def bf16(*shape):
    return jax.ShapeDtypeStruct(shape, jnp.bfloat16)


def announce(groups, bins_hbm, node_hbm, weight_hbm, label_hbm, split_hbm, out_ref, row_ref,
             near_ref, node_ref, weight_ref, label_ref, split_ref, block_ref, sems):
    copies = [
        pltpu.make_async_copy(src, dst, sems.at[k])
        for k, (src, dst) in enumerate(
            ((split_hbm, split_ref), (node_hbm, node_ref), (weight_hbm, weight_ref),
             (label_hbm, label_ref))
        )
    ]
    rows, half = near_ref.shape
    part = rows // PARTS
    first = pl.multiple_of(lax.axis_index("core") * half, half)
    slabs = [
        pltpu.make_async_copy(
            bins_hbm.at[pl.ds(k * part, part), pl.ds(first, half)],
            near_ref.at[pl.ds(k * part, part)],
            sems.at[5 + k],
        )
        for k in range(PARTS)
    ]
    for c in copies + slabs:
        c.start()
    copies[0].wait()
    split = split_ref[...].astype(jnp.float32)
    held = split.shape[0] // groups
    block = jnp.concatenate(
        [split[g * held : (g + 1) * held] for g in range(groups)], axis=1
    )
    if block.shape[1] < LANES:
        block = jnp.concatenate(
            [block, jnp.zeros((held, LANES - block.shape[1]), jnp.float32)], axis=1
        )
    many = max(1, 8 // held)
    some = jnp.concatenate([block] * many, axis=0)
    for k in range(block_ref.shape[0] // some.shape[0]):
        block_ref[k * some.shape[0] : (k + 1) * some.shape[0]] = some
    out = pltpu.make_async_copy(block_ref, out_ref, sems.at[4])
    out.start()
    for c in copies[1:]:
        c.wait()
    weight = weight_ref[...]
    row_ref[0:1] = node_ref[...].astype(jnp.float32)
    row_ref[1:2] = weight.astype(jnp.bfloat16).astype(jnp.float32)
    row_ref[2:3] = (weight * label_ref[...]).astype(jnp.bfloat16).astype(jnp.float32)
    for c in slabs:
        c.wait()
    out.wait()


def sides_of(nodes, row_ref):
    node = row_ref[0:1].astype(jnp.int32)
    hot = lax.broadcasted_iota(jnp.int32, (nodes, node.shape[1]), 0) == node
    return jnp.concatenate(
        [jnp.where(hot, row_ref[1:2], 0.0), jnp.where(hot, row_ref[2:3], 0.0)], axis=0
    ).astype(jnp.bfloat16)


def histogram(nodes, bins_ref, row_ref, before_ref, out_ref):
    half = out_ref.shape[2]
    rows, width = bins_ref.shape
    if width == half:
        bins = bins_ref[...]
    else:
        first = pl.multiple_of(lax.axis_index("core") * half, half)
        bins = bins_ref[:, pl.ds(first, half)]
    bins = bins.astype(jnp.bfloat16)
    sides = sides_of(nodes, row_ref)
    one, zero = jnp.bfloat16(1), jnp.bfloat16(0)
    for b in range(0, BINS, 2):
        acc = jnp.zeros((2 * nodes, 2 * half), jnp.float32)
        for r in range(0, rows, STEP):
            chunk = bins[r : r + STEP]
            mask = jnp.concatenate(
                [jnp.where(chunk <= jnp.bfloat16(b + k), one, zero) for k in range(2)], axis=1
            )
            acc += jnp.dot(sides[:, r : r + STEP], mask, preferred_element_type=jnp.float32)
        for k in range(2):
            here = acc[:, k * half : (k + 1) * half]
            out_ref[b + k] = here if before_ref is None else before_ref[b + k] + here


def choose(sizes, groups, held, feat_part, half_n, got_ref, below_ref, total_ref, out_ref):
    half = below_ref.shape[2]
    nodes = below_ref.shape[1] // 2
    mine = half // feat_part
    base = lax.axis_index("core") * mine
    n_near, n_line, n_chip = sizes["near"], sizes["line"], sizes["chip"]
    n_rows = sizes["far"] * n_near
    layers = []
    for z in range(n_rows):
        cols = []
        for i in range(mine):
            chip = (base + i) // 2
            d = place_in(
                FIRST, sizes, far=z // n_near, near=z % n_near,
                line=chip // n_chip, chip=chip % n_chip, core=i % 2,
            )
            cols.append(got_ref[pl.ds(d * held, held)])
        layers += [
            jnp.concatenate([c[:, g * feat_part : (g + 1) * feat_part] for c in cols], axis=1)
            for g in range(groups)
        ]
    split = jnp.concatenate(layers, axis=0)
    left0, left1 = below_ref[0, :nodes], below_ref[0, nodes:]
    for b in range(1, BINS - 1):
        further = split >= b
        left0 = jnp.where(further, below_ref[b, :nodes], left0)
        left1 = jnp.where(further, below_ref[b, nodes:], left1)
    total = total_ref[...]
    lines = 2 * half_n + 1
    for z in range(n_rows):
        for c in range(2):
            at = (z * 2 + c) * half_n
            tile = jnp.concatenate(
                [left0[at : at + half_n], left1[at : at + half_n], total], axis=0
            )
            for line in range(n_line):
                for chip in range(n_chip):
                    d = place_in(
                        SECOND, sizes, far=z // n_near, near=z % n_near,
                        line=line, chip=chip, core=c,
                    )
                    out_ref[d * lines : (d + 1) * lines] = tile


def split_gain(half_n, node_part, sizes, part_ref, gain_ref):
    lines = 2 * half_n + 1
    after = math.prod(sizes[a] for a in SECOND[SECOND.index("core") + 1 :])
    sums = []
    for c in range(2):
        both = None
        for d in range(math.prod(sizes.values())):
            if (d // after) % 2 == c:
                one = part_ref[d * lines : (d + 1) * lines]
                both = one if both is None else both + one
        sums.append(both)
    left0 = jnp.concatenate([s[:half_n] for s in sums], axis=1)
    left1 = jnp.concatenate([s[half_n : 2 * half_n] for s in sums], axis=1)
    row = sums[0][2 * half_n :]
    where = lax.axis_index(ROWS) * node_part + lax.axis_index("core") * half_n
    lane = lax.broadcasted_iota(jnp.int32, (half_n, LANES), 1)
    at = lax.broadcasted_iota(jnp.int32, (half_n, LANES), 0) + where
    total0 = jnp.sum(jnp.where(lane == at, row, 0.0), axis=1, keepdims=True)
    total1 = jnp.sum(jnp.where(lane == at + LANES // 2, row, 0.0), axis=1, keepdims=True)
    right0 = total0 - left0
    right1 = total1 - left1
    gain_ref[...] = (
        left1 * left1 / (left0 + 1.0)
        + right1 * right1 / (right0 + 1.0)
        - total1 * total1 / (total0 + 1.0)
    ) / (total0 + 1.0)


def finish(gain_ref, theirs_ref, out_ref, best_ref):
    mine, theirs = gain_ref[...], theirs_ref[...]
    first = lax.axis_index("core") == 0
    gain = jnp.concatenate(
        [jnp.where(first, mine, theirs), jnp.where(first, theirs, mine)], axis=0
    )
    n = gain.shape[0]
    best = jnp.max(gain, axis=1, keepdims=True)
    eye = lax.broadcasted_iota(jnp.int32, (n, n), 0) == lax.broadcasted_iota(jnp.int32, (n, n), 1)
    best_ref[...] = jnp.sum(jnp.where(eye, best, 0.0), axis=0, keepdims=True)
    feats, width = gain.shape[1], out_ref.shape[1]
    own = lax.axis_index(FEAT) * width
    turned = pltpu.roll(gain, lax.rem(feats - own, feats), 1)
    out_ref[...] = turned[:, : out_ref.shape[1]]


def shards(bins, node_of, weight, label, split_bins):
    sizes = {axis: lax.axis_size(axis) for axis in ALL}
    n_rows = sizes["far"] * sizes["near"]
    n_all = math.prod(sizes.values())
    rows_here, feats = bins.shape
    node_part, feat_part = split_bins.shape
    nodes = node_part * n_rows
    half_f = feats // 2
    half_n = node_part // 2
    groups = min(LANES // feat_part, node_part)
    held = node_part // groups
    lines = 2 * half_n + 1
    pair = [(0, 1), (1, 0)]
    far_bins = lax.ppermute(bins, "core", pair)
    def k_announce(*refs):
        announce(groups, *refs)
    per_row = [x.reshape(1, rows_here) for x in (node_of, weight, label)]
    block, row, near = call(
        k_announce,
        [f32(n_all * held, LANES), f32(3, rows_here),
         jax.ShapeDtypeStruct((rows_here, half_f), jnp.int32)],
        bins, *per_row, split_bins, place=[HBM] * 5, where=[HBM, VMEM, VMEM],
        scratch=[
            pltpu.VMEM((1, rows_here), jnp.int32),
            pltpu.VMEM((1, rows_here), jnp.float32),
            pltpu.VMEM((1, rows_here), jnp.float32),
            pltpu.VMEM(split_bins.shape, jnp.int32),
            pltpu.VMEM((n_all * held, LANES), jnp.float32),
            pltpu.SemaphoreType.DMA((5 + PARTS,)),
        ],
    )
    got = lax.all_to_all(
        block.reshape(n_all, 1, held * LANES), FIRST, 0, 0, tiled=True
    ).reshape(n_all * held, LANES)
    far_row = lax.ppermute(row, "core", pair)

    def k_near(bins_ref, row_ref, out_ref):
        histogram(nodes, bins_ref, row_ref, None, out_ref)
    (below,) = call(k_near, [f32(BINS, 2 * nodes, half_f)], near, row)
    def k_far(bins_ref, row_ref, before_ref, out_ref, total_ref):
        histogram(nodes, bins_ref, row_ref, before_ref, out_ref)
        everything = out_ref[BINS - 1]
        eye = lax.broadcasted_iota(jnp.int32, everything.shape, 0) == lax.broadcasted_iota(
            jnp.int32, everything.shape, 1
        )
        total_ref[...] = jnp.sum(jnp.where(eye, everything, 0.0), axis=0, keepdims=True)
    below, total = call(
        k_far, [f32(BINS, 2 * nodes, half_f), f32(1, 2 * nodes)], far_bins, far_row, below
    )

    def k_choose(*refs):
        choose(sizes, groups, held, feat_part, half_n, *refs)
    (parts,) = call(k_choose, [f32(n_all * lines, half_f)], got, below, total)
    parts = lax.all_to_all(
        parts.reshape(n_all, 1, lines * half_f), SECOND, 0, 0, tiled=True
    ).reshape(n_all * lines, half_f)

    def k_gain(*refs):
        split_gain(half_n, node_part, sizes, *refs)
    (gain,) = call(k_gain, [f32(half_n, feats)], parts)
    other = lax.ppermute(gain, "core", pair)
    out, best = call(
        finish, [f32(node_part, feat_part), f32(1, node_part)], gain, other
    )
    return out, best.reshape(node_part)


def solution(mesh):
    n_rows, n_feat = mesh.devices.shape
    cores = Mesh(mesh.devices.reshape(n_rows // 2, 2, n_feat // 4, 2, 2), ALL)
    placed = (P(ALL, None), P(ALL), P(ALL), P(ALL), P(ROWS, FEAT))
    return jax.shard_map(
        shards,
        mesh=cores,
        in_specs=placed,
        out_specs=(P(ROWS, FEAT), P(ROWS)),
        check_vma=False,
    )
```
